128 devices in a mesh: plane: 8 (over y, core), line: 16 (over x, z).
Axes of the slice: x: 4, y: 4, z: 4, core: 2. Of those that a mesh axis runs over, the one named last changes fastest.
Arguments:
- flow_state: float32 [5, 128, 2048, 128], P(None, 'plane', 'line'), may hold values from -6 to 6
- wave_speed: float32 [128, 2048, 128], P('plane', 'line'), may hold values from 0.3 to 3
- left_eig: float32 [5, 5], replicated, may hold values from -2.5 to 2.5
- right_eig: float32 [5, 5], replicated, may hold values from -2.5 to 2.5
- lower_inverse: float32 [5, 128, 2048, 128], P(None, 'plane', 'line')
- upper_inverse: float32 [5, 128, 2048, 128], P(None, 'plane', 'line')
- lower_link: float32 [3, 5, 128, 16, 128], P(None, None, 'plane', 'line'), may hold values from 0.29 to 0.33
- upper_link: float32 [3, 5, 128, 16, 128], P(None, None, 'plane', 'line'), may hold values from 0.29 to 0.33
- donor_rows: int32 [8, 16, 8, 32], P('plane', 'line'), may hold values from 0 to 1919
- stencil_offsets: int32 [8, 16, 8, 32], P('plane', 'line'), may hold values from 1 to 128, as said below
- donor_weights: float32 [2, 8, 16, 8, 32], P(None, 'plane', 'line'), may hold values from 0.2 to 0.8
- block_counts: int32 [8, 16, 8], P(None, 'line', 'plane'), may hold values from 8 to 32, as said below
- receptor_rows: int32 [8, 16, 8, 32], P('plane', 'line'), may hold values from 0 to 2047, as said below
Outputs:
- next_state: float32 [5, 128, 2048, 128], P(None, 'plane', 'line')
The draws below stay inside these ranges and needn't reach their ends.
Inputs may be any that keep to these rules, and one draw needn't show every extreme that they name: `donor_rows`: a donor row leaves room for the stencil offset inside its block. `stencil_offsets`: each offset is 1 or 128. `block_counts`: at most 32 blocks from one source block to one owner; in every line block one owner receives 32 from every source. `receptor_rows`: on each receptor block the rows of all sources and slots are distinct.
All inputs are finite; a program needn't handle non-finite values.
Results may differ from the reference program's by a relative error of at most 0.00014.
Values sent between devices are 32-bit elements; how exact they have to be, the bound alone decides.
No kernel may reach another device: no remote copies, remote signals or barrier semaphores. Data moves between devices by JAX's collectives and lax.ppermute only.
A program may use at most 128 MiB of HBM per device.

```python
import math
import jax
import jax.numpy as jnp
from jax import lax

FLOW_VARIABLES = 5
R = 128
PL_DEV = 16
LDEV = 128
CAP = 32
NPL = 128
NL = 2048
N_PLANE = 8
N_LINE = 16


def band_inverse(key, reflect):
    random_keys = jax.random.split(key, 8)
    lines = N_LINE * LDEV
    plane_list = N_PLANE * PL_DEV
    row_pos = (jnp.arange(lines, dtype=jnp.int32) % LDEV)[None, None, :, None]
    col_pos = jnp.arange(LDEV, dtype=jnp.int32)[None, None, None, :]
    if reflect:
        row_pos = LDEV - 1 - row_pos
        col_pos = LDEV - 1 - col_pos
    shape_all = (FLOW_VARIABLES, plane_list, lines, LDEV)
    spread_part = jax.random.normal(random_keys[0], shape_all, jnp.float32) * 0.4 / jnp.sqrt(row_pos.astype(jnp.float32) + 1.0)
    diagonal = jax.random.uniform(random_keys[1], (FLOW_VARIABLES, plane_list, lines, 1), jnp.float32, 1.0, 1.5)
    slow_share = 0.5
    sluggish_factor = jax.random.uniform(random_keys[2], (FLOW_VARIABLES, plane_list, 1, 1, 1), jnp.float32) < slow_share
    sluggish_retained = jax.random.uniform(random_keys[4], (FLOW_VARIABLES, plane_list, N_LINE, 1, 1), jnp.float32, 0.95, 1.0)
    quick_retained = jnp.exp(jax.random.uniform(random_keys[5], (FLOW_VARIABLES, plane_list, N_LINE, 1, 1), jnp.float32, math.log(0.05), math.log(0.3)))
    sudden_jump = jax.random.uniform(random_keys[6], (FLOW_VARIABLES, plane_list, N_LINE, 1, 1), jnp.float32) < 1.0 / N_LINE
    jump_threshold = jax.random.uniform(random_keys[7], (FLOW_VARIABLES, plane_list, N_LINE, 1, 1), jnp.float32, 0.5, 0.8)
    retained_mask = jnp.where(sluggish_factor, sluggish_retained, quick_retained) * jnp.where(sudden_jump, jump_threshold, 1.0)
    retained_mask = jnp.broadcast_to(retained_mask, (FLOW_VARIABLES, plane_list, N_LINE, LDEV, 1)).reshape(FLOW_VARIABLES, plane_list, lines, 1)
    carried = retained_mask * (1.0 + 0.03 * jax.random.normal(random_keys[3], shape_all, jnp.float32))
    below = jnp.where(col_pos < 2, carried, spread_part)
    return jnp.where(col_pos == row_pos, diagonal, jnp.where(col_pos < row_pos, below, 0.0))


def draw_lower_inverse(key, part):
    return band_inverse(jax.random.fold_in(key, 11), False)


def draw_upper_inverse(key, part):
    return band_inverse(jax.random.fold_in(key, 12), True)


def draw_stencil_offsets(key, part):
    picks = jax.random.randint(key, (N_PLANE, N_LINE, N_PLANE, CAP), 0, 2)
    return (1 + (LDEV - 1) * picks).astype(jnp.int32)


def draw_block_counts(key, part):
    random_keys = jax.random.split(jax.random.fold_in(key, 21), 2)
    base = jax.random.randint(random_keys[0], (N_PLANE, N_LINE, N_PLANE), CAP // 4, CAP // 2 + 1)
    hottest = jax.random.randint(random_keys[1], (N_LINE,), 0, N_PLANE)
    owner = jnp.arange(N_PLANE, dtype=jnp.int32)[None, None, :]
    return jnp.where(owner == hottest[None, :, None], CAP, base).astype(jnp.int32)


def first_rows(subkey):
    return jax.random.permutation(subkey, PL_DEV * LDEV)[:N_PLANE * CAP]


def draw_receptor_rows(key, part):
    random_keys = jax.random.split(jax.random.fold_in(key, 31), N_PLANE * N_LINE)
    chosen = jax.vmap(first_rows)(random_keys)
    return chosen.reshape(N_PLANE, N_LINE, N_PLANE, CAP).astype(jnp.int32)


def with_ends(result, key, smallest, high):
    longest = result.shape.index(max(result.shape))
    spots = []
    for shift in (0, 1):
        where = [jax.random.randint(jax.random.fold_in(key, axis), (), 0, length) for axis, length in enumerate(result.shape)]
        where[longest] = (where[longest] + shift) % result.shape[longest]
        spots.append(tuple(where))
    return result.at[spots[0]].set(smallest).at[spots[1]].set(high)


def shard_levels(own_key, extent, pieces, smallest, largest):
    def one(dim, shards_of):
        draws = jax.random.uniform(jax.random.fold_in(jax.random.fold_in(own_key, 6), dim), (shards_of,), jnp.float32, smallest / len(pieces), largest / len(pieces))
        return jnp.repeat(jnp.exp(draws), extent[dim] // shards_of).reshape((-1,) + (1,) * (len(extent) - dim - 1))

    gain = one(*pieces[0])
    for cut in pieces[1:]:
        gain = gain * one(*cut)
    return gain


def gaussian(rng, shape, deviation, bound, shards=(), kind=jnp.bfloat16):
    drawn = jax.random.normal(rng, shape, jnp.float32) * deviation
    if len(shards) > 0:
        drawn = shard_levels(rng, shape, shards, -0.22, 0.18) * drawn
    return jnp.clip(drawn, min=-bound, max=bound).astype(kind)


def setup_inputs(seed: int = 0) -> dict:
    arg_keys = jax.random.split(jax.random.key(seed), 14)
    flow_state = gaussian(arg_keys[0], (FLOW_VARIABLES, NPL, NL, R), 1.0, 6.0, ((1, 8), (2, 16)), jnp.float32)
    wave_speed = jnp.clip(jnp.exp(math.log(3.0) - 2.3025851 * jax.random.uniform(arg_keys[1], (NPL, NL, R), jnp.float32) ** shard_levels(arg_keys[1], (NPL, NL, R), ((0, 8), (1, 16)), -0.2, 0.2)), 0.3, 3.0)
    left_eig = gaussian(arg_keys[2], (FLOW_VARIABLES, FLOW_VARIABLES), FLOW_VARIABLES ** -0.5, 2.5, (), jnp.float32)
    right_eig = gaussian(arg_keys[3], (FLOW_VARIABLES, FLOW_VARIABLES), FLOW_VARIABLES ** -0.5, 2.5, (), jnp.float32)
    lower_inverse = draw_lower_inverse(jax.random.fold_in(arg_keys[13], 71), 0)
    upper_inverse = draw_upper_inverse(jax.random.fold_in(arg_keys[13], 71), 0)
    lower_link = jnp.clip(0.29 + 0.04000002 * jax.random.uniform(arg_keys[6], (3, FLOW_VARIABLES, NPL, N_LINE, R), jnp.float32) ** shard_levels(arg_keys[6], (3, FLOW_VARIABLES, NPL, N_LINE, R), ((2, 8), (3, 16)), -0.2, 0.2), 0.29, 0.33)
    upper_link = jnp.clip(0.29 + 0.04000002 * jax.random.uniform(arg_keys[7], (3, FLOW_VARIABLES, NPL, N_LINE, R), jnp.float32) ** shard_levels(arg_keys[7], (3, FLOW_VARIABLES, NPL, N_LINE, R), ((2, 8), (3, 16)), -0.2, 0.2), 0.29, 0.33)
    donor_rows = with_ends(jax.random.randint(arg_keys[8], (N_PLANE, N_LINE, N_PLANE, CAP), 0, (PL_DEV - 1) * LDEV), jax.random.fold_in(arg_keys[8], 1), 0, ((PL_DEV - 1) * LDEV) - 1).astype(jnp.int32)
    stencil_offsets = draw_stencil_offsets(jax.random.fold_in(arg_keys[13], 71), 0)
    donor_weights = jnp.clip(0.2 + 0.6 * jax.random.uniform(arg_keys[10], (2, N_PLANE, N_LINE, N_PLANE, CAP), jnp.float32) ** shard_levels(arg_keys[10], (2, N_PLANE, N_LINE, N_PLANE, CAP), ((1, 8), (2, 16)), -0.2, 0.2), 0.2, 0.8)
    block_counts = draw_block_counts(jax.random.fold_in(arg_keys[13], 71), 0)
    receptor_rows = draw_receptor_rows(jax.random.fold_in(arg_keys[13], 71), 0)
    return dict(flow_state=flow_state, wave_speed=wave_speed, left_eig=left_eig, right_eig=right_eig, lower_inverse=lower_inverse, upper_inverse=upper_inverse, lower_link=lower_link, upper_link=upper_link, donor_rows=donor_rows, stencil_offsets=stencil_offsets, donor_weights=donor_weights, block_counts=block_counts, receptor_rows=receptor_rows)


exact_mode = lax.Precision.HIGHEST


def tendency_of(extended, patched, wave_speed):
    along_line = extended[:, :, 3:-1] - extended[:, :, 1:-3]
    fourth = extended[:, :, 4:] - 4.0 * extended[:, :, 3:-1] + 6.0 * extended[:, :, 2:-2] - 4.0 * extended[:, :, 1:-3] + extended[:, :, :-4]
    widened = jnp.pad(patched, ((0, 0), (0, 0), (0, 0), (1, 1)))
    along_row = widened[..., 2:] - widened[..., :-2]
    return -wave_speed[None] * (0.5 * (along_line + along_row) + 0.0625 * fourth)


def place_rows(block, target, values):
    return block.at[:, target, :].set(values, mode="drop")


def reference(flow_state, wave_speed, left_eig, right_eig, lower_inverse, upper_inverse, lower_link, upper_link, donor_rows, stencil_offsets, donor_weights, block_counts, receptor_rows):
    rows_dev = PL_DEV * LDEV
    slots = N_PLANE * CAP
    plane_list = N_PLANE * PL_DEV
    blocks = flow_state.reshape(FLOW_VARIABLES, N_PLANE, PL_DEV, N_LINE, LDEV, R).transpose(1, 3, 0, 2, 4, 5).reshape(N_PLANE, N_LINE, FLOW_VARIABLES, rows_dev, R)
    shape_all = (N_PLANE, N_LINE, FLOW_VARIABLES, slots, R)
    first = jnp.broadcast_to(donor_rows.reshape(N_PLANE, N_LINE, 1, slots, 1), shape_all).astype(jnp.int32)
    second = jnp.broadcast_to((donor_rows + stencil_offsets).reshape(N_PLANE, N_LINE, 1, slots, 1), shape_all).astype(jnp.int32)
    weight_near = donor_weights[0].reshape(N_PLANE, N_LINE, 1, slots, 1)
    weight_far = donor_weights[1].reshape(N_PLANE, N_LINE, 1, slots, 1)
    donor_values = weight_near * jnp.take_along_axis(blocks, first, axis=3) + weight_far * jnp.take_along_axis(blocks, second, axis=3)
    received = donor_values.reshape(N_PLANE, N_LINE, FLOW_VARIABLES, N_PLANE, CAP, R).transpose(3, 1, 2, 0, 4, 5).reshape(N_PLANE, N_LINE, FLOW_VARIABLES, slots, R)
    counts = jnp.transpose(block_counts, (2, 1, 0))
    valid = jnp.arange(CAP, dtype=jnp.int32)[None, None, None, :] < counts[..., None]
    target = jnp.where(valid, receptor_rows, rows_dev).reshape(N_PLANE, N_LINE, slots).astype(jnp.int32)
    filled = jax.vmap(jax.vmap(place_rows))(blocks, target, received)
    patched = filled.reshape(N_PLANE, N_LINE, FLOW_VARIABLES, PL_DEV, LDEV, R).transpose(2, 0, 3, 1, 4, 5).reshape(FLOW_VARIABLES, plane_list, N_LINE * LDEV, R)
    extended = jnp.pad(patched, ((0, 0), (0, 0), (2, 2), (0, 0)))
    tendency = tendency_of(extended, patched, wave_speed)
    characteristic = jnp.einsum("vu,upnr->vpnr", left_eig, tendency, precision=exact_mode)
    lower_blocks = lower_inverse.reshape(FLOW_VARIABLES, plane_list, N_LINE, LDEV, LDEV)
    particular = jnp.einsum("vpjik,vpjkr->vpjir", lower_blocks, characteristic.reshape(FLOW_VARIABLES, plane_list, N_LINE, LDEV, R), precision=exact_mode)
    last_value = jnp.zeros((FLOW_VARIABLES, plane_list, R), jnp.float32)
    second_value = jnp.zeros((FLOW_VARIABLES, plane_list, R), jnp.float32)
    sweeps = []
    for index in range(N_LINE):
        inverse = lower_blocks[:, :, index]
        coupling = lower_link[:, :, :, index]
        first_term = (coupling[0] * last_value + coupling[1] * second_value)[:, :, None, :]
        second_term = (coupling[2] * last_value)[:, :, None, :]
        solved = particular[:, :, index] - inverse[:, :, :, 0:1] * first_term - inverse[:, :, :, 1:2] * second_term
        last_value = solved[:, :, -1]
        second_value = solved[:, :, -2]
        sweeps.append(solved)
    forward_sweep = jnp.stack(sweeps, axis=2)
    upper_blocks = upper_inverse.reshape(FLOW_VARIABLES, plane_list, N_LINE, LDEV, LDEV)
    projected = jnp.einsum("vpjik,vpjkr->vpjir", upper_blocks, forward_sweep, precision=exact_mode)
    head_value = jnp.zeros((FLOW_VARIABLES, plane_list, R), jnp.float32)
    following_value = jnp.zeros((FLOW_VARIABLES, plane_list, R), jnp.float32)
    results = []
    for index in range(N_LINE - 1, -1, -1):
        inverse = upper_blocks[:, :, index]
        coupling = upper_link[:, :, :, index]
        first_term = (coupling[0] * head_value + coupling[1] * following_value)[:, :, None, :]
        second_term = (coupling[2] * head_value)[:, :, None, :]
        solved = projected[:, :, index] - inverse[:, :, :, -1:] * first_term - inverse[:, :, :, -2:-1] * second_term
        head_value = solved[:, :, 0]
        following_value = solved[:, :, 1]
        results.insert(0, solved)
    backward_sweep = jnp.stack(results, axis=2).reshape(FLOW_VARIABLES, plane_list, N_LINE * LDEV, R)
    change = jnp.einsum("vu,upnr->vpnr", right_eig, backward_sweep, precision=exact_mode)
    return patched + change
```

```python
import functools

import jax
import jax.numpy as jnp
from jax import lax
from jax.experimental import pallas as pl
from jax.experimental.pallas import tpu as pltpu
from jax.sharding import PartitionSpec as P

F32 = jnp.float32
BF16 = jnp.bfloat16
V = 5
PL = 16
N = 128
PAD = 144
SPARE = 143
ROWS = 16
EDGES = (126, 127, 0, 1)


def split(x):
    high = x.astype(BF16)
    low = (x - high.astype(F32)).astype(BF16)
    return jnp.concatenate([high, low], axis=1)


def product(left_parts, right_parts):
    both = jnp.concatenate([right_parts, right_parts], axis=0)
    wide = jnp.dot(left_parts, both, preferred_element_type=F32)
    return wide[:, :N] + wide[:, N:]


def gather_kernel(rows, offsets, weights, flow, out):
    for d in range(8):
        for c in range(32):
            first = rows[0, 0, d, c]
            second = first + offsets[0, 0, d, c]
            out[d, 0, pl.ds(c, 1), :] = (
                weights[0, 0, 0, d, c] * flow[0, pl.ds(first, 1), :]
                + weights[1, 0, 0, d, c] * flow[0, pl.ds(second, 1), :]
            )


def gather_donors(donor_rows, stencil_offsets, donor_weights, flat):
    smem = pl.BlockSpec(memory_space=pltpu.SMEM)
    return pl.pallas_call(
        gather_kernel,
        grid=(V,),
        in_specs=[smem, smem, smem, pl.BlockSpec((1, PL * N, N), lambda v: (v, 0, 0))],
        out_specs=pl.BlockSpec((8, 1, 32, N), lambda v: (0, v, 0, 0)),
        out_shape=jax.ShapeDtypeStruct((8, V, 32, N), F32),
        cost_estimate=pl.CostEstimate(flops=10**6, bytes_accessed=6 * 10**6, transcendentals=0),
        name="gather_donors",
    )(donor_rows, stencil_offsets, donor_weights, flat)


def factors_kernel(lower, upper, both_parts, edge_rows, columns, scalars):
    lane = lax.broadcasted_iota(jnp.int32, (N, N), 1)
    lane_row = lax.broadcasted_iota(jnp.int32, (1, N), 1)
    cols = jnp.zeros((N, N), F32)
    for v in range(V):
        low, up = lower[v, 0], upper[v, 0]
        both = product(split(up), split(low))
        both_parts[v, 0] = split(both)
        edge_rows[v, 0] = split(
            jnp.concatenate([both[0:2], low[126:128], jnp.zeros((12, N), F32)], axis=0)
        )
        at = 4 * v
        cols = jnp.where((lane >= at) & (lane < at + 4), pltpu.roll(both, at + 2, axis=1), cols)
        at = 20 + 2 * v
        cols = jnp.where((lane >= at) & (lane < at + 2), pltpu.roll(up, at + 2, axis=1), cols)
        packed = jnp.zeros((1, N), F32)
        for i, row in enumerate((both[0:1], both[1:2], low[126:127], low[127:128])):
            at = 4 * i
            packed = jnp.where(
                (lane_row >= at) & (lane_row < at + 4), pltpu.roll(row, at + 2, axis=1), packed
            )
        for i, row in enumerate((up[0:1], up[1:2])):
            at = 16 + 2 * i
            packed = jnp.where(
                (lane_row >= at) & (lane_row < at + 2), pltpu.roll(row, at + 2, axis=1), packed
            )
        scalars[0, pl.ds(v, 1), :] = packed
    high = cols.astype(BF16).astype(F32)
    pair = high + pltpu.roll(cols - high, 32, axis=1)
    columns[0] = (pair + pltpu.roll(pair, 64, axis=1)).astype(BF16)


def factors(lower_inverse, upper_inverse):
    block = pl.BlockSpec((V, 1, N, N), lambda p: (0, p, 0, 0))
    return pl.pallas_call(
        factors_kernel,
        grid=(PL,),
        in_specs=[block, block],
        out_specs=[
            pl.BlockSpec((V, 1, N, 2 * N), lambda p: (0, p, 0, 0)),
            pl.BlockSpec((V, 1, 16, 2 * N), lambda p: (0, p, 0, 0)),
            pl.BlockSpec((1, N, N), lambda p: (p, 0, 0)),
            pl.BlockSpec((1, 8, N), lambda p: (p, 0, 0)),
        ],
        out_shape=[
            jax.ShapeDtypeStruct((V, PL, N, 2 * N), BF16),
            jax.ShapeDtypeStruct((V, PL, 16, 2 * N), BF16),
            jax.ShapeDtypeStruct((PL, N, N), BF16),
            jax.ShapeDtypeStruct((PL, 8, N), F32),
        ],
        cost_estimate=pl.CostEstimate(
            flops=2 * 10**9, bytes_accessed=17 * 10**6, transcendentals=0
        ),
        name="factors",
    )(lower_inverse, upper_inverse)


def stencil_kernel(
    target, left_eig, received, flow, wave, edge_rows, scalars, lower_link, upper_link,
    char_parts, patched, edges, grid_rows, load_sem, store_sem,
):
    p = pl.program_id(0)

    def loads(v):
        return pltpu.make_async_copy(flow.at[v], grid_rows.at[v, :, pl.ds(8, N), :], load_sem.at[v])

    def stores(v):
        return pltpu.make_async_copy(
            grid_rows.at[v, :, pl.ds(8, N), :], patched.at[v], store_sem.at[v]
        )

    @pl.when(p == 0)
    def _():
        for v in range(V):
            loads(v).start()
        zeros = jnp.zeros((8, N), F32)
        for v in range(V):
            for q in range(PL):
                grid_rows[v, q, 0:8, :] = zeros
                grid_rows[v, q, 136:144, :] = zeros
        for v in range(V):
            loads(v).wait()
        for d in range(8):
            for c in range(32):
                row = target[d, c]
                plane = lax.shift_right_logical(row, 8)
                point = lax.bitwise_and(row, 255)
                for v in range(V):
                    grid_rows[v, plane, pl.ds(point, 1), :] = received[d, v, pl.ds(c, 1), :]
        for v in range(V):
            stores(v).start()

    lane = lax.broadcasted_iota(jnp.int32, (32, N), 1)
    for start in range(0, N, 32):
        tendency = []
        for v in range(V):
            at = lambda shift: grid_rows[v, p, pl.ds(8 + start + shift, 32), :]
            here = at(0)
            after = jnp.where(lane == N - 1, 0.0, pltpu.roll(here, N - 1, axis=1))
            before = jnp.where(lane == 0, 0.0, pltpu.roll(here, 1, axis=1))
            tendency.append(
                (at(2) + at(-2))
                + 4.0 * (at(1) - 3.0 * at(-1) + 1.5 * here)
                + 8.0 * (after - before)
            )
        speed = -0.0625 * wave[0, pl.ds(start, 32), :]
        tendency = [speed * x for x in tendency]
        for v in range(V):
            total = left_eig[v, 0] * tendency[0]
            for u in range(1, V):
                total = total + left_eig[v, u] * tendency[u]
            char_parts[v, 0, pl.ds(start, 32), :] = split(total)
    for v in range(V):
        base = v * ROWS
        found = product(edge_rows[v, 0], char_parts[v, 0])
        edges[0, base : base + 4, :] = found[0:4]
        edges[0, base + 4 : base + 6, :] = grid_rows[v, p, 134:136, :]
        edges[0, base + 6 : base + 8, :] = grid_rows[v, p, 8:10, :]
        for k in range(3):
            edges[0, base + 8 + k : base + 9 + k, :] = lower_link[k, v, pl.ds(p, 1), :]
            edges[0, base + 11 + k : base + 12 + k, :] = upper_link[k, v, pl.ds(p, 1), :]
        point = EDGES[min(v, 3)]
        edges[0, base + 14 : base + 15, :] = wave[0, point : point + 1, :]
        edges[0, base + 15 : base + 16, :] = scalars[0, v : v + 1, :]

    @pl.when(p == PL - 1)
    def _():
        for v in range(V):
            stores(v).wait()


def stencil(target, left_eig, received, flow, wave, edge_rows, scalars, lower_link, upper_link):
    smem = pl.BlockSpec(memory_space=pltpu.SMEM)
    whole = lambda *shape: pl.BlockSpec(shape, lambda p: (0,) * len(shape))
    return pl.pallas_call(
        stencil_kernel,
        grid=(PL,),
        in_specs=[
            smem,
            smem,
            whole(8, V, 32, N),
            pl.BlockSpec(memory_space=pl.ANY),
            pl.BlockSpec((1, N, N), lambda p: (p, 0, 0)),
            pl.BlockSpec((V, 1, 16, 2 * N), lambda p: (0, p, 0, 0)),
            pl.BlockSpec((1, 8, N), lambda p: (p, 0, 0)),
            whole(3, V, PL, N),
            whole(3, V, PL, N),
        ],
        out_specs=[
            pl.BlockSpec((V, 1, N, 2 * N), lambda p: (0, p, 0, 0)),
            pl.BlockSpec(memory_space=pl.ANY),
            pl.BlockSpec((1, V * ROWS, N), lambda p: (p, 0, 0)),
        ],
        out_shape=[
            jax.ShapeDtypeStruct((V, PL, N, 2 * N), BF16),
            jax.ShapeDtypeStruct((V, PL, N, N), F32),
            jax.ShapeDtypeStruct((PL, V * ROWS, N), F32),
        ],
        scratch_shapes=[
            pltpu.VMEM((V, PL, PAD, N), F32),
            pltpu.SemaphoreType.DMA((V,)),
            pltpu.SemaphoreType.DMA((V,)),
        ],
        compiler_params=pltpu.CompilerParams(vmem_limit_bytes=16 * 2**20),
        cost_estimate=pl.CostEstimate(
            flops=10**8, bytes_accessed=18 * 10**6, transcendentals=0
        ),
        name="stencil",
    )(target, left_eig, received, flow, wave, edge_rows, scalars, lower_link, upper_link)


def uncoupled_kernel(right_eig, both_parts, char_parts, patched, out):
    solved = [product(both_parts[v, 0], char_parts[v, 0]) for v in range(V)]
    for u in range(V):
        total = patched[u, 0]
        for v in range(V):
            total = total + right_eig[u, v] * solved[v]
        out[u, 0] = total


def uncoupled(right_eig, both_parts, char_parts, patched):
    parts = pl.BlockSpec((V, 1, N, 2 * N), lambda p: (0, p, 0, 0))
    block = pl.BlockSpec((V, 1, N, N), lambda p: (0, p, 0, 0))
    return pl.pallas_call(
        uncoupled_kernel,
        grid=(PL,),
        in_specs=[pl.BlockSpec(memory_space=pltpu.SMEM), parts, parts, block],
        out_specs=block,
        out_shape=jax.ShapeDtypeStruct((V, PL, N, N), F32),
        cost_estimate=pl.CostEstimate(
            flops=2 * 10**9, bytes_accessed=21 * 10**6, transcendentals=0
        ),
        name="uncoupled",
    )(right_eig, both_parts, char_parts, patched)


def sweep_kernel(blocks, left_eig, got, out):
    take = lambda l, j: got[l, pl.ds(j, V, stride=ROWS), :]
    zero = jnp.zeros((V, N), F32)
    eig = [jnp.broadcast_to(left_eig[:, u : u + 1], (V, N)) for u in range(V)]

    def mixed(tendency):
        total = eig[0] * tendency[0:1]
        for u in range(1, V):
            total = total + eig[u] * tendency[u : u + 1]
        return total

    first, second = zero, zero
    offsets = []
    factor_up = []
    for l in range(blocks):
        speed = {e: -0.0625 * got[l, ROWS * i + 14 : ROWS * i + 15, :] for i, e in enumerate(EDGES)}
        packed = take(l, 15)
        scalar = lambda k: packed[:, k : k + 1]
        edge = {e: zero for e in EDGES}
        if l > 0:
            far, near = take(l - 1, 4), take(l - 1, 5)
            edge[0] = mixed(speed[0] * (far - 12.0 * near))
            edge[1] = mixed(speed[1] * near)
        if l < blocks - 1:
            near, far = take(l + 1, 6), take(l + 1, 7)
            edge[126] = mixed(speed[126] * near)
            edge[127] = mixed(speed[127] * (far + 4.0 * near))
        edge[0] = edge[0] - (take(l, 8) * first + take(l, 9) * second)
        edge[1] = edge[1] - take(l, 10) * first
        for i, e in enumerate(EDGES):
            out[l, pl.ds(i, V, stride=4), :] = edge[e]
        found = []
        for j in range(4):
            total = take(l, j)
            for i, e in enumerate(EDGES):
                total = total + scalar(4 * j + i) * edge[e]
            found.append(total)
        offsets.append(found[:2])
        first, second = found[3], found[2]
    first, second = zero, zero
    for l in range(blocks - 1, -1, -1):
        packed = take(l, 15)
        last = -(take(l, 11) * first + take(l, 12) * second)
        before = -(take(l, 13) * first)
        out[l, pl.ds(20, V, stride=2), :] = before
        out[l, pl.ds(21, V, stride=2), :] = last
        out[l, 30:32, :] = jnp.zeros((2, N), F32)
        first, second = [
            offsets[l][j] + packed[:, 16 + 2 * j : 17 + 2 * j] * before
            + packed[:, 17 + 2 * j : 18 + 2 * j] * last
            for j in range(2)
        ]


def sweeps(left_eig, got):
    blocks = got.shape[0]
    vmem = pl.BlockSpec(memory_space=pltpu.VMEM)
    return pl.pallas_call(
        functools.partial(sweep_kernel, blocks),
        in_specs=[vmem, vmem],
        out_specs=vmem,
        out_shape=jax.ShapeDtypeStruct((blocks, 32, N), F32),
        name="sweeps",
    )(left_eig, got)


def coupled_kernel(right_eig, base, columns, incoming, out, pattern):
    @pl.when(pl.program_id(0) == 0)
    def _():
        for u in range(V):
            for v in range(V):
                pattern[u, 4 * v : 4 * v + 4, :] = jnp.full((4, N), right_eig[u, v])
                pattern[u, 20 + 2 * v : 22 + 2 * v, :] = jnp.full((2, N), right_eig[u, v])
            pattern[u, 30:32, :] = jnp.zeros((2, N), F32)

    sides = []
    for u in range(V):
        scaled = incoming[0] * pattern[u]
        high = scaled.astype(BF16)
        low = (scaled - high.astype(F32)).astype(BF16)
        sides.append(jnp.concatenate([high, high, low, low], axis=0))
    change = jnp.dot(columns[0], jnp.concatenate(sides, axis=1), preferred_element_type=F32)
    for u in range(V):
        out[u, 0] = base[u, 0] + change[:, u * N : (u + 1) * N]


def coupled(right_eig, base, columns, incoming):
    block = pl.BlockSpec((V, 1, N, N), lambda p: (0, p, 0, 0))
    return pl.pallas_call(
        coupled_kernel,
        grid=(PL,),
        in_specs=[
            pl.BlockSpec(memory_space=pltpu.SMEM),
            block,
            pl.BlockSpec((1, N, N), lambda p: (p, 0, 0)),
            pl.BlockSpec((1, 32, N), lambda p: (p, 0, 0)),
        ],
        out_specs=block,
        out_shape=jax.ShapeDtypeStruct((V, PL, N, N), F32),
        scratch_shapes=[pltpu.VMEM((V, 32, N), F32)],
        name="coupled",
    )(right_eig, base, columns, incoming)


def local(
    flow_state,
    wave_speed,
    left_eig,
    right_eig,
    lower_inverse,
    upper_inverse,
    lower_link,
    upper_link,
    donor_rows,
    stencil_offsets,
    donor_weights,
    block_counts,
    receptor_rows,
):
    flat = flow_state.reshape(V, PL * N, N)
    outgoing = gather_donors(donor_rows, stencil_offsets, donor_weights, flat)
    received = lax.all_to_all(outgoing, "plane", 0, 0, tiled=True)
    rows = receptor_rows.reshape(8, 32)
    valid = jnp.arange(32, dtype=jnp.int32)[None, :] < block_counts.reshape(8, 1)
    target = jnp.where(valid, (rows // N) * 256 + rows % N + 8, SPARE)
    both_parts, edge_rows, columns, scalars = factors(lower_inverse, upper_inverse)
    char_parts, patched, edges = stencil(
        target,
        left_eig,
        received,
        flow_state,
        wave_speed,
        edge_rows,
        scalars,
        lower_link.reshape(3, V, PL, N),
        upper_link.reshape(3, V, PL, N),
    )
    got = lax.all_to_all(edges, "line", 0, 0, tiled=True)
    base = uncoupled(right_eig, both_parts, char_parts, patched)
    incoming = lax.all_to_all(sweeps(left_eig, got), "line", 0, 0, tiled=True)
    return coupled(right_eig, base, columns, incoming)


def solution(mesh):
    in_specs = (
        P(None, "plane", "line", None),
        P("plane", "line", None),
        P(),
        P(),
        P(None, "plane", "line", None),
        P(None, "plane", "line", None),
        P(None, None, "plane", "line", None),
        P(None, None, "plane", "line", None),
        P("plane", "line", None, None),
        P("plane", "line", None, None),
        P(None, "plane", "line", None, None),
        P(None, "line", "plane"),
        P("plane", "line", None, None),
    )
    out_specs = P(None, "plane", "line", None)
    return jax.shard_map(local, mesh=mesh, in_specs=in_specs, out_specs=out_specs, check_vma=False)
```

```python
import functools

import jax
import jax.numpy as jnp
from jax import lax
from jax.experimental import pallas as pl
from jax.experimental.pallas import tpu as pltpu
from jax.sharding import PartitionSpec as P

F32 = jnp.float32
BF16 = jnp.bfloat16
V = 5
PL = 16
N = 128
PAD = 144
SPARE = 143
ROWS = 16
EDGES = (126, 127, 0, 1)
PAIR = 2
GROUPS = PL // PAIR
AHEAD = 3
SCALARS = pl.BlockSpec(memory_space=pltpu.SMEM)
RESIDENT = pl.BlockSpec(memory_space=pltpu.VMEM)
OUTSIDE = pl.BlockSpec(memory_space=pl.ANY)


def room(mebibytes):
    return pltpu.CompilerParams(vmem_limit_bytes=mebibytes * 2**20)


def in_hbm(x):
    return pltpu.with_memory_space_constraint(x, pltpu.HBM)


def split(x):
    high = x.astype(BF16)
    low = (x - high.astype(F32)).astype(BF16)
    return jnp.concatenate([high, low], axis=1)


def product(left_parts, right_parts):
    both = jnp.concatenate([right_parts, right_parts], axis=0)
    wide = jnp.dot(left_parts, both, preferred_element_type=F32)
    return wide[:, :N] + wide[:, N:]


def gather_kernel(rows, offsets, weights, flow, out, held, sem):
    def load(v):
        return pltpu.make_async_copy(flow.at[v], held.at[v], sem.at[v])

    for v in range(V):
        load(v).start()
    for group in ((0, 1), (2, 3, 4)):
        for v in group:
            load(v).wait()

        def peer(d, _):
            for c in range(32):
                first = rows[0, 0, d, c]
                second = first + offsets[0, 0, d, c]
                near, far = weights[0, 0, 0, d, c], weights[1, 0, 0, d, c]
                for v in group:
                    out[d, v, pl.ds(c, 1), :] = (
                        near * held[v, pl.ds(first, 1), :] + far * held[v, pl.ds(second, 1), :]
                    )
            return 0

        lax.fori_loop(0, 8, peer, 0)


def gather_donors(donor_rows, stencil_offsets, donor_weights, flat):
    return pl.pallas_call(
        gather_kernel,
        in_specs=[SCALARS, SCALARS, SCALARS, OUTSIDE],
        out_specs=RESIDENT,
        out_shape=jax.ShapeDtypeStruct((8, V, 32, N), F32),
        scratch_shapes=[pltpu.VMEM((V, PL * N, N), F32), pltpu.SemaphoreType.DMA((V,))],
        compiler_params=room(56),
        cost_estimate=pl.CostEstimate(flops=10**6, bytes_accessed=6 * 10**6, transcendentals=0),
        name="gather_donors",
    )(donor_rows, stencil_offsets, donor_weights, in_hbm(flat))


def factors_kernel(
    lower, upper, both_out, edge_rows, columns, scalars,
    lows, ups, both_parts, load_sem, store_sem,
):
    def loads(g):
        planes = pl.ds(g * PAIR, PAIR)
        return [
            pltpu.make_async_copy(source.at[:, planes], held.at[:, planes], load_sem.at[k, g])
            for k, (source, held) in enumerate(((lower, lows), (upper, ups)))
        ]

    def store(g):
        planes = pl.ds(g * PAIR, PAIR)
        return pltpu.make_async_copy(
            both_parts.at[:, planes], both_out.at[:, planes], store_sem.at[g]
        )

    for g in range(AHEAD):
        for copy in loads(g):
            copy.start()
    lane = lax.broadcasted_iota(jnp.int32, (N, N), 1)
    lane_row = lax.broadcasted_iota(jnp.int32, (1, N), 1)

    def group(g, _):
        @pl.when(g + AHEAD < GROUPS)
        def _():
            for copy in loads(g + AHEAD):
                copy.start()

        for copy in loads(g):
            copy.wait()
        for q in range(PAIR):
            p = g * PAIR + q
            cols = jnp.zeros((N, N), F32)
            for v in range(V):
                low, up = lows[v, p], ups[v, p]
                both = product(split(up), split(low))
                both_parts[v, p] = split(both)
                four = jnp.concatenate([both[0:2], low[126:128]], axis=0)
                high = four.astype(BF16).astype(F32)
                edge_rows[v, p] = jnp.concatenate(
                    [high, four - high, jnp.zeros((8, N), F32)], axis=0
                ).astype(BF16)
                at = 4 * v
                cols = jnp.where((lane >= at) & (lane < at + 4), pltpu.roll(both, at + 2, axis=1), cols)
                at = 20 + 2 * v
                cols = jnp.where((lane >= at) & (lane < at + 2), pltpu.roll(up, at + 2, axis=1), cols)
                packed = jnp.zeros((1, N), F32)
                for i, row in enumerate((both[0:1], both[1:2], low[126:127], low[127:128])):
                    at = 4 * i
                    packed = jnp.where(
                        (lane_row >= at) & (lane_row < at + 4), pltpu.roll(row, at + 2, axis=1), packed
                    )
                for i, row in enumerate((up[0:1], up[1:2])):
                    at = 16 + 2 * i
                    packed = jnp.where(
                        (lane_row >= at) & (lane_row < at + 2), pltpu.roll(row, at + 2, axis=1), packed
                    )
                scalars[p, pl.ds(v, 1), :] = packed
            high = cols.astype(BF16).astype(F32)
            pair = high + pltpu.roll(cols - high, 32, axis=1)
            columns[p] = (pair + pltpu.roll(pair, 64, axis=1)).astype(BF16)
        store(g).start()
        return 0

    lax.fori_loop(0, GROUPS, group, 0)
    for g in range(GROUPS):
        store(g).wait()


def factors(lower_inverse, upper_inverse):
    return pl.pallas_call(
        factors_kernel,
        in_specs=[OUTSIDE] * 2,
        out_specs=[OUTSIDE] + [RESIDENT] * 3,
        out_shape=[
            pltpu.HBM((V, PL, N, 2 * N), BF16),
            jax.ShapeDtypeStruct((V, PL, 16, N), BF16),
            pltpu.HBM((PL, N, N), BF16),
            jax.ShapeDtypeStruct((PL, 8, N), F32),
        ],
        scratch_shapes=[
            pltpu.VMEM((V, PL, N, N), F32),
            pltpu.VMEM((V, PL, N, N), F32),
            pltpu.VMEM((V, PL, N, 2 * N), BF16),
            pltpu.SemaphoreType.DMA((2, GROUPS)),
            pltpu.SemaphoreType.DMA((GROUPS,)),
        ],
        compiler_params=room(32),
        cost_estimate=pl.CostEstimate(
            flops=2 * 10**9, bytes_accessed=17 * 10**6, transcendentals=0
        ),
        name="factors",
    )(in_hbm(lower_inverse), in_hbm(upper_inverse))


def stencil_kernel(
    target, left_eig, received, flow, wave, edge_rows, scalars, lower_link, upper_link,
    char_out, patched, edges, grid_rows, char_parts, load_sem, char_sem, patch_sem,
):
    def load(v):
        return pltpu.make_async_copy(flow.at[v], grid_rows.at[v, :, pl.ds(8, N), :], load_sem.at[v])

    def store_char(p):
        return pltpu.make_async_copy(char_parts.at[:, p], char_out.at[:, p], char_sem.at[p])

    def store_patched(v):
        return pltpu.make_async_copy(
            grid_rows.at[v, :, pl.ds(8, N), :], patched.at[v], patch_sem.at[v]
        )

    for v in range(V):
        load(v).start()
    zeros = jnp.zeros((8, N), F32)
    for v in range(V):
        for q in range(PL):
            grid_rows[v, q, 0:8, :] = zeros
            grid_rows[v, q, 136:144, :] = zeros
    for group in ((0, 1), (2, 3), (4,)):
        for v in group:
            load(v).wait()

        def place(d, _):
            for c in range(32):
                row = target[d, c]
                plane = lax.shift_right_logical(row, 8)
                point = lax.bitwise_and(row, 255)
                for v in group:
                    grid_rows[v, plane, pl.ds(point, 1), :] = received[d, v, pl.ds(c, 1), :]
            return 0

        lax.fori_loop(0, 8, place, 0)
        for v in group:
            store_patched(v).start()
    lane = lax.broadcasted_iota(jnp.int32, (32, N), 1)

    def characteristic(p):
        for start in range(0, N, 32):
            tendency = []
            for v in range(V):
                at = lambda shift: grid_rows[v, p, pl.ds(8 + start + shift, 32), :]
                here = at(0)
                after = jnp.where(lane == N - 1, 0.0, pltpu.roll(here, N - 1, axis=1))
                before = jnp.where(lane == 0, 0.0, pltpu.roll(here, 1, axis=1))
                tendency.append(
                    (at(2) + at(-2))
                    + 4.0 * (at(1) - 3.0 * at(-1) + 1.5 * here)
                    + 8.0 * (after - before)
                )
            speed = -0.0625 * wave[p, pl.ds(start, 32), :]
            tendency = [speed * x for x in tendency]
            for v in range(V):
                total = left_eig[v, 0] * tendency[0]
                for u in range(1, V):
                    total = total + left_eig[v, u] * tendency[u]
                char_parts[v, p, pl.ds(start, 32), :] = split(total)

    def block_edges(p):
        for v in range(V):
            base = v * ROWS
            wide = jnp.dot(edge_rows[v, p], char_parts[v, p], preferred_element_type=F32)
            found = wide[:, :N] + wide[:, N:]
            edges[p, base : base + 4, :] = found[0:4] + found[4:8]
            edges[p, base + 4 : base + 6, :] = grid_rows[v, p, 134:136, :]
            edges[p, base + 6 : base + 8, :] = grid_rows[v, p, 8:10, :]
            for k in range(3):
                edges[p, base + 8 + k : base + 9 + k, :] = lower_link[k, v, pl.ds(p, 1), :]
                edges[p, base + 11 + k : base + 12 + k, :] = upper_link[k, v, pl.ds(p, 1), :]
            point = EDGES[min(v, 3)]
            edges[p, base + 14 : base + 15, :] = wave[p, point : point + 1, :]
            edges[p, base + 15 : base + 16, :] = scalars[p, v : v + 1, :]

    def step(p, _):
        block_edges(p - 1)
        characteristic(p)
        store_char(p).start()
        return 0

    characteristic(0)
    store_char(0).start()
    lax.fori_loop(1, PL, step, 0)
    block_edges(PL - 1)
    for p in range(PL):
        store_char(p).wait()
    for v in range(V):
        store_patched(v).wait()


def stencil(target, left_eig, received, flow, wave, edge_rows, scalars, lower_link, upper_link):
    return pl.pallas_call(
        stencil_kernel,
        in_specs=[SCALARS, SCALARS, RESIDENT, OUTSIDE] + [RESIDENT] * 5,
        out_specs=[OUTSIDE, OUTSIDE, RESIDENT],
        out_shape=[
            pltpu.HBM((V, PL, N, 2 * N), BF16),
            pltpu.HBM((V, PL, N, N), F32),
            jax.ShapeDtypeStruct((PL, V * ROWS, N), F32),
        ],
        scratch_shapes=[
            pltpu.VMEM((V, PL, PAD, N), F32),
            pltpu.VMEM((V, PL, N, 2 * N), BF16),
            pltpu.SemaphoreType.DMA((V,)),
            pltpu.SemaphoreType.DMA((PL,)),
            pltpu.SemaphoreType.DMA((V,)),
        ],
        compiler_params=room(32),
        cost_estimate=pl.CostEstimate(
            flops=10**8, bytes_accessed=18 * 10**6, transcendentals=0
        ),
        name="stencil",
    )(
        target, left_eig, received, in_hbm(flow), wave, edge_rows, scalars, lower_link, upper_link
    )


def uncoupled_kernel(
    right_eig, both_in, char_in, patched_in, out, both_parts, char_parts, base, sem, store_sem
):
    def loads(g):
        planes = pl.ds(g * PAIR, PAIR)
        return [
            pltpu.make_async_copy(source.at[:, planes], held.at[:, planes], sem.at[k, g])
            for k, (source, held) in enumerate(
                ((both_in, both_parts), (char_in, char_parts), (patched_in, base))
            )
        ]

    def store(g):
        planes = pl.ds(g * PAIR, PAIR)
        return pltpu.make_async_copy(base.at[:, planes], out.at[:, planes], store_sem.at[g])

    for g in range(AHEAD):
        for copy in loads(g):
            copy.start()

    def group(g, _):
        @pl.when(g + AHEAD < GROUPS)
        def _():
            for copy in loads(g + AHEAD):
                copy.start()

        for copy in loads(g):
            copy.wait()
        for q in range(PAIR):
            p = g * PAIR + q
            solved = [product(both_parts[v, p], char_parts[v, p]) for v in range(V)]
            for u in range(V):
                total = base[u, p]
                for v in range(V):
                    total = total + right_eig[u, v] * solved[v]
                base[u, p] = total
        store(g).start()
        return 0

    lax.fori_loop(0, GROUPS, group, 0)
    for g in range(GROUPS):
        store(g).wait()


def uncoupled(right_eig, both_parts, char_parts, patched):
    return pl.pallas_call(
        uncoupled_kernel,
        in_specs=[SCALARS, OUTSIDE, OUTSIDE, OUTSIDE],
        out_specs=OUTSIDE,
        out_shape=pltpu.HBM((V, PL, N, N), F32),
        scratch_shapes=[
            pltpu.VMEM((V, PL, N, 2 * N), BF16),
            pltpu.VMEM((V, PL, N, 2 * N), BF16),
            pltpu.VMEM((V, PL, N, N), F32),
            pltpu.SemaphoreType.DMA((3, GROUPS)),
            pltpu.SemaphoreType.DMA((GROUPS,)),
        ],
        compiler_params=room(32),
        cost_estimate=pl.CostEstimate(
            flops=2 * 10**9, bytes_accessed=21 * 10**6, transcendentals=0
        ),
        name="uncoupled",
    )(right_eig, in_hbm(both_parts), in_hbm(char_parts), in_hbm(patched))


def sweep_kernel(blocks, left_eig, got, out):
    take = lambda l, j: got[l, pl.ds(j, V, stride=ROWS), :]
    zero = jnp.zeros((V, N), F32)
    eig = [jnp.broadcast_to(left_eig[:, u : u + 1], (V, N)) for u in range(V)]

    def mixed(tendency):
        total = eig[0] * tendency[0:1]
        for u in range(1, V):
            total = total + eig[u] * tendency[u : u + 1]
        return total

    first, second = zero, zero
    offsets = []
    factor_up = []
    for l in range(blocks):
        speed = {e: -0.0625 * got[l, ROWS * i + 14 : ROWS * i + 15, :] for i, e in enumerate(EDGES)}
        packed = take(l, 15)
        scalar = lambda k: packed[:, k : k + 1]
        edge = {e: zero for e in EDGES}
        if l > 0:
            far, near = take(l - 1, 4), take(l - 1, 5)
            edge[0] = mixed(speed[0] * (far - 12.0 * near))
            edge[1] = mixed(speed[1] * near)
        if l < blocks - 1:
            near, far = take(l + 1, 6), take(l + 1, 7)
            edge[126] = mixed(speed[126] * near)
            edge[127] = mixed(speed[127] * (far + 4.0 * near))
        edge[0] = edge[0] - (take(l, 8) * first + take(l, 9) * second)
        edge[1] = edge[1] - take(l, 10) * first
        for i, e in enumerate(EDGES):
            out[l, pl.ds(i, V, stride=4), :] = edge[e]
        found = []
        for j in range(4):
            total = take(l, j)
            for i, e in enumerate(EDGES):
                total = total + scalar(4 * j + i) * edge[e]
            found.append(total)
        offsets.append(found[:2])
        first, second = found[3], found[2]
    first, second = zero, zero
    for l in range(blocks - 1, -1, -1):
        packed = take(l, 15)
        last = -(take(l, 11) * first + take(l, 12) * second)
        before = -(take(l, 13) * first)
        out[l, pl.ds(20, V, stride=2), :] = before
        out[l, pl.ds(21, V, stride=2), :] = last
        out[l, 30:32, :] = jnp.zeros((2, N), F32)
        first, second = [
            offsets[l][j] + packed[:, 16 + 2 * j : 17 + 2 * j] * before
            + packed[:, 17 + 2 * j : 18 + 2 * j] * last
            for j in range(2)
        ]


def sweeps(left_eig, got):
    blocks = got.shape[0]
    return pl.pallas_call(
        functools.partial(sweep_kernel, blocks),
        in_specs=[RESIDENT, RESIDENT],
        out_specs=RESIDENT,
        out_shape=jax.ShapeDtypeStruct((blocks, 32, N), F32),
        compiler_params=room(32),
        name="sweeps",
    )(left_eig, got)


def coupled_kernel(right_eig, base, columns, incoming, out, held, pattern, load_sem, sem):
    def load(g):
        planes = pl.ds(g * PAIR, PAIR)
        return pltpu.make_async_copy(base.at[:, planes], held.at[:, planes], load_sem.at[g])

    def store(g):
        planes = pl.ds(g * PAIR, PAIR)
        return pltpu.make_async_copy(held.at[:, planes], out.at[:, planes], sem.at[g])

    for g in range(GROUPS):
        load(g).start()
    for u in range(V):
        for v in range(V):
            pattern[u, 4 * v : 4 * v + 4, :] = jnp.full((4, N), right_eig[u, v])
            pattern[u, 20 + 2 * v : 22 + 2 * v, :] = jnp.full((2, N), right_eig[u, v])
        pattern[u, 30:32, :] = jnp.zeros((2, N), F32)

    def group(g, _):
        load(g).wait()
        for q in range(PAIR):
            p = g * PAIR + q
            sides = []
            for u in range(V):
                scaled = incoming[p] * pattern[u]
                high = scaled.astype(BF16)
                low = (scaled - high.astype(F32)).astype(BF16)
                sides.append(jnp.concatenate([high, high, low, low], axis=0))
            change = jnp.dot(columns[p], jnp.concatenate(sides, axis=1), preferred_element_type=F32)
            for u in range(V):
                held[u, p] = held[u, p] + change[:, u * N : (u + 1) * N]
        store(g).start()
        return 0

    lax.fori_loop(0, GROUPS, group, 0)
    for g in range(GROUPS):
        store(g).wait()


def coupled(right_eig, base, columns, incoming):
    return pl.pallas_call(
        coupled_kernel,
        in_specs=[SCALARS, OUTSIDE, RESIDENT, RESIDENT],
        out_specs=OUTSIDE,
        out_shape=pltpu.HBM((V, PL, N, N), F32),
        scratch_shapes=[
            pltpu.VMEM((V, PL, N, N), F32),
            pltpu.VMEM((V, 32, N), F32),
            pltpu.SemaphoreType.DMA((GROUPS,)),
            pltpu.SemaphoreType.DMA((GROUPS,)),
        ],
        compiler_params=room(32),
        name="coupled",
    )(right_eig, in_hbm(base), columns, incoming)


def local(
    flow_state,
    wave_speed,
    left_eig,
    right_eig,
    lower_inverse,
    upper_inverse,
    lower_link,
    upper_link,
    donor_rows,
    stencil_offsets,
    donor_weights,
    block_counts,
    receptor_rows,
):
    flat = flow_state.reshape(V, PL * N, N)
    outgoing = gather_donors(donor_rows, stencil_offsets, donor_weights, flat)
    received = lax.all_to_all(outgoing, "plane", 0, 0, tiled=True)
    rows = receptor_rows.reshape(8, 32)
    valid = jnp.arange(32, dtype=jnp.int32)[None, :] < block_counts.reshape(8, 1)
    target = jnp.where(valid, (rows // N) * 256 + rows % N + 8, SPARE)
    lower_inverse, outgoing = lax.optimization_barrier((lower_inverse, outgoing))
    both_parts, edge_rows, columns, scalars = factors(lower_inverse, upper_inverse)
    char_parts, patched, edges = stencil(
        target,
        left_eig,
        received,
        flow_state,
        wave_speed,
        edge_rows,
        scalars,
        lower_link.reshape(3, V, PL, N),
        upper_link.reshape(3, V, PL, N),
    )
    got = lax.all_to_all(edges, "line", 0, 0, tiled=True)
    solved = sweeps(left_eig, got)
    incoming = lax.all_to_all(solved, "line", 0, 0, tiled=True)
    char_parts, _ = lax.optimization_barrier((char_parts, solved))
    base = uncoupled(right_eig, both_parts, char_parts, patched)
    return coupled(right_eig, base, columns, incoming)


def solution(mesh):
    in_specs = (
        P(None, "plane", "line", None),
        P("plane", "line", None),
        P(),
        P(),
        P(None, "plane", "line", None),
        P(None, "plane", "line", None),
        P(None, None, "plane", "line", None),
        P(None, None, "plane", "line", None),
        P("plane", "line", None, None),
        P("plane", "line", None, None),
        P(None, "plane", "line", None, None),
        P(None, "line", "plane"),
        P("plane", "line", None, None),
    )
    out_specs = P(None, "plane", "line", None)
    return jax.shard_map(local, mesh=mesh, in_specs=in_specs, out_specs=out_specs, check_vma=False)
```

```python
import functools

import jax
import jax.numpy as jnp
from jax import lax
from jax.experimental import pallas as pl
from jax.experimental.pallas import tpu as pltpu
from jax.sharding import PartitionSpec as P

F32 = jnp.float32
BF16 = jnp.bfloat16
V = 5
PL = 16
N = 128
PAD = 144
SPARE = 143
ROWS = 16
EDGES = (126, 127, 0, 1)
PAIR = 2
GROUPS = PL // PAIR
AHEAD = 3
SCALARS = pl.BlockSpec(memory_space=pltpu.SMEM)
RESIDENT = pl.BlockSpec(memory_space=pltpu.VMEM)
OUTSIDE = pl.BlockSpec(memory_space=pl.ANY)


def room(mebibytes):
    return pltpu.CompilerParams(vmem_limit_bytes=mebibytes * 2**20)


def in_hbm(x):
    return pltpu.with_memory_space_constraint(x, pltpu.HBM)


def split(x):
    high = x.astype(BF16)
    low = (x - high.astype(F32)).astype(BF16)
    return jnp.concatenate([high, low], axis=1)


def product(left_parts, right_parts):
    both = jnp.concatenate([right_parts, right_parts], axis=0)
    wide = jnp.dot(left_parts, both, preferred_element_type=F32)
    return wide[:, :N] + wide[:, N:]


def gather_kernel(rows, offsets, weights, flow, out, held, found, sem, store_sem):
    groups = ((0, 1), (2, 3, 4))

    def load(v):
        return pltpu.make_async_copy(flow.at[v], held.at[v], sem.at[v])

    def store(d, k):
        part = pl.ds(groups[k][0], len(groups[k]))
        return pltpu.make_async_copy(found.at[d, part], out.at[d, part], store_sem.at[k, d])

    for v in range(V):
        load(v).start()
    for k, group in enumerate(groups):
        for v in group:
            load(v).wait()

        def peer(d, _):
            for c in range(32):
                first = rows[0, 0, d, c]
                second = first + offsets[0, 0, d, c]
                near, far = weights[0, 0, 0, d, c], weights[1, 0, 0, d, c]
                for v in group:
                    found[d, v, pl.ds(c, 1), :] = (
                        near * held[v, pl.ds(first, 1), :] + far * held[v, pl.ds(second, 1), :]
                    )
            store(d, k).start()
            return 0

        lax.fori_loop(0, 8, peer, 0)
    for k in range(2):
        for d in range(8):
            store(d, k).wait()


def gather_donors(donor_rows, stencil_offsets, donor_weights, flat):
    return pl.pallas_call(
        gather_kernel,
        in_specs=[SCALARS, SCALARS, SCALARS, OUTSIDE],
        out_specs=OUTSIDE,
        out_shape=pltpu.HBM((8, V, 32, N), F32),
        scratch_shapes=[
            pltpu.VMEM((V, PL * N, N), F32),
            pltpu.VMEM((8, V, 32, N), F32),
            pltpu.SemaphoreType.DMA((V,)),
            pltpu.SemaphoreType.DMA((2, 8)),
        ],
        compiler_params=room(56),
        cost_estimate=pl.CostEstimate(flops=10**6, bytes_accessed=6 * 10**6, transcendentals=0),
        name="gather_donors",
    )(donor_rows, stencil_offsets, donor_weights, in_hbm(flat))


def factors_kernel(
    lower, upper, both_out, edge_rows, columns, scalars,
    lows, ups, both_parts, load_sem, store_sem,
):
    def loads(g):
        planes = pl.ds(g * PAIR, PAIR)
        return [
            pltpu.make_async_copy(source.at[:, planes], held.at[:, planes], load_sem.at[k, g])
            for k, (source, held) in enumerate(((lower, lows), (upper, ups)))
        ]

    def store(g):
        planes = pl.ds(g * PAIR, PAIR)
        return pltpu.make_async_copy(
            both_parts.at[:, planes], both_out.at[:, planes], store_sem.at[g]
        )

    for g in range(AHEAD):
        for copy in loads(g):
            copy.start()
    lane = lax.broadcasted_iota(jnp.int32, (N, N), 1)
    lane_row = lax.broadcasted_iota(jnp.int32, (1, N), 1)

    def group(g, _):
        @pl.when(g + AHEAD < GROUPS)
        def _():
            for copy in loads(g + AHEAD):
                copy.start()

        for copy in loads(g):
            copy.wait()
        for q in range(PAIR):
            p = g * PAIR + q
            cols = jnp.zeros((N, N), F32)
            ends = []
            for v in range(V):
                low, up = lows[v, p], ups[v, p]
                both = product(split(up), split(low))
                both_parts[v, p] = split(both)
                ends += [both[0:2], low[126:128]]
                at = 4 * v
                cols = jnp.where((lane >= at) & (lane < at + 4), pltpu.roll(both, at + 2, axis=1), cols)
                at = 20 + 2 * v
                cols = jnp.where((lane >= at) & (lane < at + 2), pltpu.roll(up, at + 2, axis=1), cols)
                packed = jnp.zeros((1, N), F32)
                for i, row in enumerate((both[0:1], both[1:2], low[126:127], low[127:128])):
                    at = 4 * i
                    packed = jnp.where(
                        (lane_row >= at) & (lane_row < at + 4), pltpu.roll(row, at + 2, axis=1), packed
                    )
                for i, row in enumerate((up[0:1], up[1:2])):
                    at = 16 + 2 * i
                    packed = jnp.where(
                        (lane_row >= at) & (lane_row < at + 2), pltpu.roll(row, at + 2, axis=1), packed
                    )
                scalars[p, pl.ds(v, 1), :] = packed
            ends = jnp.concatenate(ends + [jnp.zeros((4, N), F32)], axis=0)
            high = ends.astype(BF16).astype(F32)
            edge_rows[p] = jnp.concatenate([high, ends - high], axis=0).astype(BF16)
            high = cols.astype(BF16).astype(F32)
            pair = high + pltpu.roll(cols - high, 32, axis=1)
            columns[p] = (pair + pltpu.roll(pair, 64, axis=1)).astype(BF16)
        store(g).start()
        return 0

    lax.fori_loop(0, GROUPS, group, 0)
    for g in range(GROUPS):
        store(g).wait()


def factors(lower_inverse, upper_inverse):
    return pl.pallas_call(
        factors_kernel,
        in_specs=[OUTSIDE] * 2,
        out_specs=[OUTSIDE] + [RESIDENT] * 3,
        out_shape=[
            pltpu.HBM((V, PL, N, 2 * N), BF16),
            jax.ShapeDtypeStruct((PL, 48, N), BF16),
            pltpu.HBM((PL, N, N), BF16),
            jax.ShapeDtypeStruct((PL, 8, N), F32),
        ],
        scratch_shapes=[
            pltpu.VMEM((V, PL, N, N), F32),
            pltpu.VMEM((V, PL, N, N), F32),
            pltpu.VMEM((V, PL, N, 2 * N), BF16),
            pltpu.SemaphoreType.DMA((2, GROUPS)),
            pltpu.SemaphoreType.DMA((GROUPS,)),
        ],
        compiler_params=room(32),
        cost_estimate=pl.CostEstimate(
            flops=2 * 10**9, bytes_accessed=17 * 10**6, transcendentals=0
        ),
        name="factors",
    )(in_hbm(lower_inverse), in_hbm(upper_inverse))


def stencil_kernel(
    target, left_eig, received, flow, wave, edge_rows, scalars, lower_link, upper_link,
    tend_out, patched, edges_out, grid_rows, tend, parts, pattern, edges,
    load_sem, tend_sem, patch_sem, edge_sem,
):
    def load(v):
        return pltpu.make_async_copy(flow.at[v], grid_rows.at[v, :, pl.ds(8, N), :], load_sem.at[v])

    def store_tend(p):
        return pltpu.make_async_copy(tend.at[:, p], tend_out.at[:, p], tend_sem.at[p])

    def store_edges(p):
        return pltpu.make_async_copy(edges.at[p], edges_out.at[p], edge_sem.at[p])

    def store_patched(v):
        return pltpu.make_async_copy(
            grid_rows.at[v, :, pl.ds(8, N), :], patched.at[v], patch_sem.at[v]
        )

    for v in range(V):
        load(v).start()
    for u in range(V):
        for v in range(V):
            pattern[u, 4 * v : 4 * v + 4, :] = jnp.full((4, N), left_eig[v, u])
        pattern[u, 20:24, :] = jnp.zeros((4, N), F32)
    zeros = jnp.zeros((8, N), F32)
    for v in range(V):
        for q in range(PL):
            grid_rows[v, q, 0:8, :] = zeros
            grid_rows[v, q, 136:144, :] = zeros
    for group in ((0, 1), (2, 3), (4,)):
        for v in group:
            load(v).wait()

        def place(d, _):
            for c in range(32):
                row = target[d, c]
                plane = lax.shift_right_logical(row, 8)
                point = lax.bitwise_and(row, 255)
                for v in group:
                    grid_rows[v, plane, pl.ds(point, 1), :] = received[d, v, pl.ds(c, 1), :]
            return 0

        lax.fori_loop(0, 8, place, 0)
        for v in group:
            store_patched(v).start()
    lane = lax.broadcasted_iota(jnp.int32, (32, N), 1)

    def tendency(p):
        for start in range(0, N, 32):
            speed = -0.0625 * wave[p, pl.ds(start, 32), :]
            for v in range(V):
                at = lambda shift: grid_rows[v, p, pl.ds(8 + start + shift, 32), :]
                here = at(0)
                after = jnp.where(lane == N - 1, 0.0, pltpu.roll(here, N - 1, axis=1))
                before = jnp.where(lane == 0, 0.0, pltpu.roll(here, 1, axis=1))
                near = (at(1) - 3.0 * at(-1)) + (1.5 * here + 2.0 * (after - before))
                total = speed * ((at(2) + at(-2)) + 4.0 * near)
                tend[v, p, pl.ds(start, 32), :] = total
                parts[lax.rem(p, 2), v, pl.ds(start, 32), :] = split(total)

    def block_edges(p):
        total = jnp.zeros((24, N), F32)
        for u in range(V):
            wide = jnp.dot(
                edge_rows[p], parts[lax.rem(p, 2), u], preferred_element_type=F32
            )
            found = wide[:, :N] + wide[:, N:]
            total = total + pattern[u] * (found[:24] + found[24:])
        for v in range(V):
            base = v * ROWS
            edges[p, base : base + 4, :] = total[4 * v : 4 * v + 4]
            edges[p, base + 4 : base + 6, :] = grid_rows[v, p, 134:136, :]
            edges[p, base + 6 : base + 8, :] = grid_rows[v, p, 8:10, :]
            for k in range(3):
                edges[p, base + 8 + k : base + 9 + k, :] = lower_link[k, v, pl.ds(p, 1), :]
                edges[p, base + 11 + k : base + 12 + k, :] = upper_link[k, v, pl.ds(p, 1), :]
            point = EDGES[min(v, 3)]
            edges[p, base + 14 : base + 15, :] = wave[p, point : point + 1, :]
            edges[p, base + 15 : base + 16, :] = scalars[p, v : v + 1, :]
        store_edges(p).start()

    def step(p, _):
        block_edges(p - 1)
        tendency(p)
        store_tend(p).start()
        return 0

    tendency(0)
    store_tend(0).start()
    lax.fori_loop(1, PL, step, 0)
    block_edges(PL - 1)
    for p in range(PL):
        store_tend(p).wait()
        store_edges(p).wait()
    for v in range(V):
        store_patched(v).wait()


def stencil(target, left_eig, received, flow, wave, edge_rows, scalars, lower_link, upper_link):
    return pl.pallas_call(
        stencil_kernel,
        in_specs=[SCALARS, SCALARS, RESIDENT, OUTSIDE] + [RESIDENT] * 5,
        out_specs=[OUTSIDE] * 3,
        out_shape=[
            pltpu.HBM((V, PL, N, N), F32),
            pltpu.HBM((V, PL, N, N), F32),
            pltpu.HBM((PL, V * ROWS, N), F32),
        ],
        scratch_shapes=[
            pltpu.VMEM((V, PL, PAD, N), F32),
            pltpu.VMEM((V, PL, N, N), F32),
            pltpu.VMEM((2, V, N, 2 * N), BF16),
            pltpu.VMEM((V, 24, N), F32),
            pltpu.VMEM((PL, V * ROWS, N), F32),
            pltpu.SemaphoreType.DMA((V,)),
            pltpu.SemaphoreType.DMA((PL,)),
            pltpu.SemaphoreType.DMA((V,)),
            pltpu.SemaphoreType.DMA((PL,)),
        ],
        compiler_params=room(32),
        cost_estimate=pl.CostEstimate(
            flops=10**8, bytes_accessed=18 * 10**6, transcendentals=0
        ),
        name="stencil",
    )(
        target, left_eig, received, in_hbm(flow), wave, edge_rows, scalars, lower_link, upper_link
    )


def uncoupled_kernel(
    left_eig, right_eig, both_in, tend_in, patched_in, out, both_parts, tend, base, sem, store_sem
):
    def loads(g):
        planes = pl.ds(g * PAIR, PAIR)
        return [
            pltpu.make_async_copy(source.at[:, planes], held.at[:, planes], sem.at[k, g])
            for k, (source, held) in enumerate(
                ((both_in, both_parts), (tend_in, tend), (patched_in, base))
            )
        ]

    def store(g):
        planes = pl.ds(g * PAIR, PAIR)
        return pltpu.make_async_copy(base.at[:, planes], out.at[:, planes], store_sem.at[g])

    for g in range(AHEAD):
        for copy in loads(g):
            copy.start()

    def group(g, _):
        @pl.when(g + AHEAD < GROUPS)
        def _():
            for copy in loads(g + AHEAD):
                copy.start()

        for copy in loads(g):
            copy.wait()
        for q in range(PAIR):
            p = g * PAIR + q
            solved = []
            for v in range(V):
                total = left_eig[v, 0] * tend[0, p]
                for u in range(1, V):
                    total = total + left_eig[v, u] * tend[u, p]
                solved.append(product(both_parts[v, p], split(total)))
            for u in range(V):
                total = base[u, p]
                for v in range(V):
                    total = total + right_eig[u, v] * solved[v]
                base[u, p] = total
        store(g).start()
        return 0

    lax.fori_loop(0, GROUPS, group, 0)
    for g in range(GROUPS):
        store(g).wait()


def uncoupled(left_eig, right_eig, both_parts, tend, patched):
    return pl.pallas_call(
        uncoupled_kernel,
        in_specs=[SCALARS, SCALARS, OUTSIDE, OUTSIDE, OUTSIDE],
        out_specs=OUTSIDE,
        out_shape=pltpu.HBM((V, PL, N, N), F32),
        scratch_shapes=[
            pltpu.VMEM((V, PL, N, 2 * N), BF16),
            pltpu.VMEM((V, PL, N, N), F32),
            pltpu.VMEM((V, PL, N, N), F32),
            pltpu.SemaphoreType.DMA((3, GROUPS)),
            pltpu.SemaphoreType.DMA((GROUPS,)),
        ],
        compiler_params=room(32),
        cost_estimate=pl.CostEstimate(
            flops=2 * 10**9, bytes_accessed=21 * 10**6, transcendentals=0
        ),
        name="uncoupled",
    )(left_eig, right_eig, in_hbm(both_parts), in_hbm(tend), in_hbm(patched))


def sweep_kernel(blocks, left_eig, got, out):
    take = lambda l, j: got[l, pl.ds(j, V, stride=ROWS), :]
    zero = jnp.zeros((V, N), F32)
    eig = [jnp.broadcast_to(left_eig[:, u : u + 1], (V, N)) for u in range(V)]

    def mixed(tendency):
        total = eig[0] * tendency[0:1]
        for u in range(1, V):
            total = total + eig[u] * tendency[u : u + 1]
        return total

    first, second = zero, zero
    offsets = []
    factor_up = []
    for l in range(blocks):
        speed = {e: -0.0625 * got[l, ROWS * i + 14 : ROWS * i + 15, :] for i, e in enumerate(EDGES)}
        packed = take(l, 15)
        scalar = lambda k: packed[:, k : k + 1]
        edge = {e: zero for e in EDGES}
        if l > 0:
            far, near = take(l - 1, 4), take(l - 1, 5)
            edge[0] = mixed(speed[0] * (far - 12.0 * near))
            edge[1] = mixed(speed[1] * near)
        if l < blocks - 1:
            near, far = take(l + 1, 6), take(l + 1, 7)
            edge[126] = mixed(speed[126] * near)
            edge[127] = mixed(speed[127] * (far + 4.0 * near))
        edge[0] = edge[0] - (take(l, 8) * first + take(l, 9) * second)
        edge[1] = edge[1] - take(l, 10) * first
        for i, e in enumerate(EDGES):
            out[l, pl.ds(i, V, stride=4), :] = edge[e]
        found = []
        for j in range(4):
            total = take(l, j)
            for i, e in enumerate(EDGES):
                total = total + scalar(4 * j + i) * edge[e]
            found.append(total)
        offsets.append(found[:2])
        first, second = found[3], found[2]
    first, second = zero, zero
    for l in range(blocks - 1, -1, -1):
        packed = take(l, 15)
        last = -(take(l, 11) * first + take(l, 12) * second)
        before = -(take(l, 13) * first)
        out[l, pl.ds(20, V, stride=2), :] = before
        out[l, pl.ds(21, V, stride=2), :] = last
        out[l, 30:32, :] = jnp.zeros((2, N), F32)
        first, second = [
            offsets[l][j] + packed[:, 16 + 2 * j : 17 + 2 * j] * before
            + packed[:, 17 + 2 * j : 18 + 2 * j] * last
            for j in range(2)
        ]


def sweeps(left_eig, got):
    blocks = got.shape[0]
    return pl.pallas_call(
        functools.partial(sweep_kernel, blocks),
        in_specs=[RESIDENT, RESIDENT],
        out_specs=RESIDENT,
        out_shape=jax.ShapeDtypeStruct((blocks, 32, N), F32),
        cost_estimate=pl.CostEstimate(
            flops=2 * 10**9, bytes_accessed=30 * 10**6, transcendentals=0
        ),
        compiler_params=room(32),
        name="sweeps",
    )(left_eig, got)


def coupled_kernel(right_eig, base, columns, incoming, out, held, pattern, sem):
    def store(g):
        planes = pl.ds(g * PAIR, PAIR)
        return pltpu.make_async_copy(held.at[:, planes], out.at[:, planes], sem.at[g])

    for u in range(V):
        for v in range(V):
            pattern[u, 4 * v : 4 * v + 4, :] = jnp.full((4, N), right_eig[u, v])
            pattern[u, 20 + 2 * v : 22 + 2 * v, :] = jnp.full((2, N), right_eig[u, v])
        pattern[u, 30:32, :] = jnp.zeros((2, N), F32)

    def group(g, _):
        for q in range(PAIR):
            p = g * PAIR + q
            sides = []
            for u in range(V):
                scaled = incoming[p] * pattern[u]
                high = scaled.astype(BF16)
                low = (scaled - high.astype(F32)).astype(BF16)
                sides.append(jnp.concatenate([high, high, low, low], axis=0))
            change = jnp.dot(columns[p], jnp.concatenate(sides, axis=1), preferred_element_type=F32)
            for u in range(V):
                held[u, p] = base[u, p] + change[:, u * N : (u + 1) * N]
        store(g).start()
        return 0

    lax.fori_loop(0, GROUPS, group, 0)
    for g in range(GROUPS):
        store(g).wait()


def coupled(right_eig, base, columns, incoming):
    return pl.pallas_call(
        coupled_kernel,
        in_specs=[SCALARS, RESIDENT, RESIDENT, RESIDENT],
        out_specs=OUTSIDE,
        out_shape=pltpu.HBM((V, PL, N, N), F32),
        scratch_shapes=[
            pltpu.VMEM((V, PL, N, N), F32),
            pltpu.VMEM((V, 32, N), F32),
            pltpu.SemaphoreType.DMA((GROUPS,)),
        ],
        compiler_params=room(32),
        name="coupled",
    )(right_eig, base, columns, incoming)


def local(
    flow_state,
    wave_speed,
    left_eig,
    right_eig,
    lower_inverse,
    upper_inverse,
    lower_link,
    upper_link,
    donor_rows,
    stencil_offsets,
    donor_weights,
    block_counts,
    receptor_rows,
):
    flat = flow_state.reshape(V, PL * N, N)
    outgoing = gather_donors(donor_rows, stencil_offsets, donor_weights, flat)
    received = lax.all_to_all(outgoing, "plane", 0, 0, tiled=True)
    rows = receptor_rows.reshape(8, 32)
    valid = jnp.arange(32, dtype=jnp.int32)[None, :] < block_counts.reshape(8, 1)
    target = jnp.where(valid, (rows // N) * 256 + rows % N + 8, SPARE)
    lower_inverse, outgoing = lax.optimization_barrier((lower_inverse, outgoing))
    both_parts, edge_rows, columns, scalars = factors(lower_inverse, upper_inverse)
    tend, patched, edges = stencil(
        target,
        left_eig,
        received,
        flow_state,
        wave_speed,
        edge_rows,
        scalars,
        lower_link.reshape(3, V, PL, N),
        upper_link.reshape(3, V, PL, N),
    )
    got = lax.all_to_all(edges, "line", 0, 0, tiled=True)
    base = uncoupled(left_eig, right_eig, both_parts, tend, patched)
    got, base = lax.optimization_barrier((got, base))
    incoming = lax.all_to_all(sweeps(left_eig, got), "line", 0, 0, tiled=True)
    return coupled(right_eig, base, columns, incoming)


def solution(mesh):
    in_specs = (
        P(None, "plane", "line", None),
        P("plane", "line", None),
        P(),
        P(),
        P(None, "plane", "line", None),
        P(None, "plane", "line", None),
        P(None, None, "plane", "line", None),
        P(None, None, "plane", "line", None),
        P("plane", "line", None, None),
        P("plane", "line", None, None),
        P(None, "plane", "line", None, None),
        P(None, "line", "plane"),
        P("plane", "line", None, None),
    )
    out_specs = P(None, "plane", "line", None)
    return jax.shard_map(local, mesh=mesh, in_specs=in_specs, out_specs=out_specs, check_vma=False)
```

```python
import functools

import jax
import jax.numpy as jnp
from jax import lax
from jax.experimental import pallas as pl
from jax.experimental.pallas import tpu as pltpu
from jax.sharding import PartitionSpec as P

F32 = jnp.float32
BF16 = jnp.bfloat16
V = 5
PL = 16
N = 128
PAD = 144
SPARE = 143
ROWS = 16
EDGES = (126, 127, 0, 1)
PAIR = 2
GROUPS = PL // PAIR
VARIABLE_GROUPS = ((0, 1), (2, 3, 4))
BATCH = 4
AHEAD = 3
SCALARS = pl.BlockSpec(memory_space=pltpu.SMEM)
RESIDENT = pl.BlockSpec(memory_space=pltpu.VMEM)
OUTSIDE = pl.BlockSpec(memory_space=pl.ANY)


def room(mebibytes):
    return pltpu.CompilerParams(vmem_limit_bytes=mebibytes * 2**20)


def in_hbm(x):
    return pltpu.with_memory_space_constraint(x, pltpu.HBM)


def split(x):
    high = x.astype(BF16)
    low = (x - high.astype(F32)).astype(BF16)
    return jnp.concatenate([high, low], axis=1)


def product(left_parts, right_parts):
    both = jnp.concatenate([right_parts, right_parts], axis=0)
    wide = jnp.dot(left_parts, both, preferred_element_type=F32)
    return wide[:, :N] + wide[:, N:]


def gather_kernel(
    rows_in, offsets_in, weights_in, flow, out,
    rows, offsets, weights, held, found, scalar_sem, sem, store_sem,
):
    groups = ((0, 1), (2, 3, 4))
    scalars = [
        pltpu.make_async_copy(source, to, scalar_sem.at[i])
        for i, (source, to) in enumerate(
            ((rows_in, rows), (offsets_in, offsets), (weights_in, weights))
        )
    ]
    for copy in scalars:
        copy.start()

    def load(v):
        return pltpu.make_async_copy(flow.at[v], held.at[v], sem.at[v])

    def store(d, k):
        part = pl.ds(groups[k][0], len(groups[k]))
        return pltpu.make_async_copy(found.at[d, part], out.at[d, part], store_sem.at[k, d])

    for v in range(V):
        load(v).start()
    for copy in scalars:
        copy.wait()
    for k, group in enumerate(groups):
        for v in group:
            load(v).wait()

        def peer(d, _):
            for c in range(32):
                first = rows[0, 0, d, c]
                second = first + offsets[0, 0, d, c]
                near, far = weights[0, 0, 0, d, c], weights[1, 0, 0, d, c]
                for v in group:
                    found[d, v, pl.ds(c, 1), :] = (
                        near * held[v, pl.ds(first, 1), :] + far * held[v, pl.ds(second, 1), :]
                    )
            store(d, k).start()
            return 0

        lax.fori_loop(0, 8, peer, 0)
    for k in range(2):
        for d in range(8):
            store(d, k).wait()


def gather_donors(donor_rows, stencil_offsets, donor_weights, flat):
    return pl.pallas_call(
        gather_kernel,
        in_specs=[OUTSIDE] * 4,
        out_specs=OUTSIDE,
        out_shape=pltpu.HBM((8, V, 32, N), F32),
        scratch_shapes=[
            pltpu.SMEM((1, 1, 8, 32), jnp.int32),
            pltpu.SMEM((1, 1, 8, 32), jnp.int32),
            pltpu.SMEM((2, 1, 1, 8, 32), F32),
            pltpu.VMEM((V, PL * N, N), F32),
            pltpu.VMEM((8, V, 32, N), F32),
            pltpu.SemaphoreType.DMA((3,)),
            pltpu.SemaphoreType.DMA((V,)),
            pltpu.SemaphoreType.DMA((2, 8)),
        ],
        compiler_params=room(56),
        cost_estimate=pl.CostEstimate(flops=10**6, bytes_accessed=6 * 10**6, transcendentals=0),
        name="gather_donors",
    )(donor_rows, stencil_offsets, donor_weights, in_hbm(flat))


def factors_kernel(
    lower, upper, wave, lower_link, upper_link, right_eig,
    both_out, edge_rows, columns, early, pattern,
    lows, ups, both_parts, load_sem, store_sem,
):
    def loads(g):
        planes = pl.ds(g * PAIR, PAIR)
        return [
            pltpu.make_async_copy(source.at[:, planes], held.at[:, planes], load_sem.at[k, g])
            for k, (source, held) in enumerate(((lower, lows), (upper, ups)))
        ]

    def store(g):
        planes = pl.ds(g * PAIR, PAIR)
        return pltpu.make_async_copy(
            both_parts.at[:, planes], both_out.at[:, planes], store_sem.at[g]
        )

    for g in range(AHEAD):
        for copy in loads(g):
            copy.start()
    for u in range(V):
        for v in range(V):
            pattern[u, 4 * v : 4 * v + 4, :] = jnp.full((4, N), right_eig[u, v])
            pattern[u, 20 + 2 * v : 22 + 2 * v, :] = jnp.full((2, N), right_eig[u, v])
        pattern[u, 30:32, :] = jnp.zeros((2, N), F32)
    lane = lax.broadcasted_iota(jnp.int32, (N, N), 1)
    lane_row = lax.broadcasted_iota(jnp.int32, (1, N), 1)

    def group(g, _):
        @pl.when(g + AHEAD < GROUPS)
        def _():
            for copy in loads(g + AHEAD):
                copy.start()

        for copy in loads(g):
            copy.wait()
        for q in range(PAIR):
            p = g * PAIR + q
            cols = jnp.zeros((N, N), F32)
            ends = []
            for v in range(V):
                low, up = lows[v, p], ups[v, p]
                both = product(split(up), split(low))
                both_parts[v, p] = split(both)
                ends += [both[0:2], low[126:128]]
                at = 4 * v
                cols = jnp.where((lane >= at) & (lane < at + 4), pltpu.roll(both, at + 2, axis=1), cols)
                at = 20 + 2 * v
                cols = jnp.where((lane >= at) & (lane < at + 2), pltpu.roll(up, at + 2, axis=1), cols)
                packed = jnp.zeros((1, N), F32)
                for i, row in enumerate((both[0:1], both[1:2], low[126:127], low[127:128])):
                    at = 4 * i
                    packed = jnp.where(
                        (lane_row >= at) & (lane_row < at + 4), pltpu.roll(row, at + 2, axis=1), packed
                    )
                for i, row in enumerate((up[0:1], up[1:2])):
                    at = 16 + 2 * i
                    packed = jnp.where(
                        (lane_row >= at) & (lane_row < at + 2), pltpu.roll(row, at + 2, axis=1), packed
                    )
                for i in range(3):
                    early[p, v, i : i + 1, :] = lower_link[i, v, pl.ds(p, 1), :]
                    early[p, v, 3 + i : 4 + i, :] = upper_link[i, v, pl.ds(p, 1), :]
                point = EDGES[min(v, 3)]
                early[p, v, 6:7, :] = wave[p, point : point + 1, :]
                early[p, v, 7:8, :] = packed
            ends = jnp.concatenate(ends + [jnp.zeros((4, N), F32)], axis=0)
            high = ends.astype(BF16).astype(F32)
            edge_rows[p] = jnp.concatenate([high, ends - high], axis=0).astype(BF16)
            high = cols.astype(BF16).astype(F32)
            pair = high + pltpu.roll(cols - high, 32, axis=1)
            columns[p] = (pair + pltpu.roll(pair, 64, axis=1)).astype(BF16)
        store(g).start()
        return 0

    lax.fori_loop(0, GROUPS, group, 0)
    for g in range(GROUPS):
        store(g).wait()


def factors(lower_inverse, upper_inverse, wave, lower_link, upper_link, right_eig):
    return pl.pallas_call(
        factors_kernel,
        in_specs=[OUTSIDE] * 2 + [RESIDENT] * 3 + [SCALARS],
        out_specs=[OUTSIDE] + [RESIDENT] * 4,
        out_shape=[
            pltpu.HBM((V, PL, N, 2 * N), BF16),
            jax.ShapeDtypeStruct((PL, 48, N), BF16),
            pltpu.HBM((PL, N, N), BF16),
            jax.ShapeDtypeStruct((PL, V, 8, N), F32),
            pltpu.HBM((V, 32, N), F32),
        ],
        scratch_shapes=[
            pltpu.VMEM((V, PL, N, N), F32),
            pltpu.VMEM((V, PL, N, N), F32),
            pltpu.VMEM((V, PL, N, 2 * N), BF16),
            pltpu.SemaphoreType.DMA((2, GROUPS)),
            pltpu.SemaphoreType.DMA((GROUPS,)),
        ],
        compiler_params=room(32),
        cost_estimate=pl.CostEstimate(
            flops=2 * 10**9, bytes_accessed=17 * 10**6, transcendentals=0
        ),
        name="factors",
    )(
        in_hbm(lower_inverse), in_hbm(upper_inverse), wave, lower_link, upper_link, right_eig
    )


def stencil_kernel(
    target_in, eig_in, received, flow, wave, edge_rows, early,
    tend_out, patched, edges_out,
    target, left_eig, grid_rows, tend, parts, pattern, sums, edges,
    scalar_sem, load_sem, tend_sem, patch_sem, edge_sem, early_sem,
):
    def load(v):
        return pltpu.make_async_copy(flow.at[v], grid_rows.at[v, :, pl.ds(8, N), :], load_sem.at[v])

    def store_tend(k, p):
        part = pl.ds(VARIABLE_GROUPS[k][0], len(VARIABLE_GROUPS[k]))
        return pltpu.make_async_copy(tend.at[part, p], tend_out.at[part, p], tend_sem.at[k, p])

    def store_edges(p):
        return pltpu.make_async_copy(edges.at[p], edges_out.at[p, :, 0], edge_sem.at[p])

    def store_patched(v):
        return pltpu.make_async_copy(
            grid_rows.at[v, :, pl.ds(8, N), :], patched.at[v], patch_sem.at[v]
        )

    copies = [
        pltpu.make_async_copy(target_in, target, scalar_sem.at[0]),
        pltpu.make_async_copy(eig_in, left_eig, scalar_sem.at[1]),
    ]
    for copy in copies:
        copy.start()
    for v in range(V):
        load(v).start()
    store_early = pltpu.make_async_copy(early, edges_out.at[:, :, 1], early_sem.at[0])
    store_early.start()
    flat_rows = grid_rows.reshape(V, PL * PAD, N)
    zeros = jnp.zeros((8, N), F32)
    for v in range(V):
        for q in range(PL):
            grid_rows[v, q, 0:8, :] = zeros
            grid_rows[v, q, 136:144, :] = zeros
    for copy in copies:
        copy.wait()
    for u in range(V):
        for v in range(V):
            pattern[u, 4 * v : 4 * v + 4, :] = jnp.full((4, N), left_eig[v, u])
        pattern[u, 20:24, :] = jnp.zeros((4, N), F32)
    lane = lax.broadcasted_iota(jnp.int32, (32, N), 1)

    for k, group in enumerate(VARIABLE_GROUPS):
        first, last = k == 0, k == len(VARIABLE_GROUPS) - 1
        for v in group:
            load(v).wait()

        def place(d, _):
            for c in range(32):
                row = target[d, c]
                for v in group:
                    flat_rows[v, pl.ds(row, 1), :] = received[d, v, pl.ds(c, 1), :]
            return 0

        lax.fori_loop(0, 8, place, 0)
        for v in group:
            store_patched(v).start()

        def tendency(p, slot):
            for start in range(0, N, 32):
                speed = -0.0625 * wave[p, pl.ds(start, 32), :]
                for v in group:
                    at = lambda shift: grid_rows[v, p, pl.ds(8 + start + shift, 32), :]
                    here = at(0)
                    after = jnp.where(lane == N - 1, 0.0, pltpu.roll(here, N - 1, axis=1))
                    before = jnp.where(lane == 0, 0.0, pltpu.roll(here, 1, axis=1))
                    near = (at(1) - 3.0 * at(-1)) + (1.5 * here + 2.0 * (after - before))
                    total = speed * ((at(2) + at(-2)) + 4.0 * near)
                    tend[v, p, pl.ds(start, 32), :] = total
                    parts[slot, v, pl.ds(start, 32), :] = split(total)
            store_tend(k, p).start()

        def block_edges(p, slot):
            total = jnp.zeros((24, N), F32) if first else sums[p]
            for u in group:
                wide = jnp.dot(
                    edge_rows[p], parts[slot, u], preferred_element_type=F32
                )
                found = wide[:, :N] + wide[:, N:]
                total = total + pattern[u] * (found[:24] + found[24:])
            if not last:
                sums[p] = total
            for v in group:
                edges[p, v, 4:6, :] = grid_rows[v, p, 134:136, :]
                edges[p, v, 6:8, :] = grid_rows[v, p, 8:10, :]
            if last:
                for v in range(V):
                    edges[p, v, 0:4, :] = total[4 * v : 4 * v + 4]
                store_edges(p).start()

        def step(i, _):
            before, now = lax.rem(i + 1, 2) * BATCH, lax.rem(i, 2) * BATCH
            for q in range(BATCH):
                block_edges((i - 1) * BATCH + q, before + q)
            for q in range(BATCH):
                tendency(i * BATCH + q, now + q)
            return 0

        for q in range(BATCH):
            tendency(q, q)
        lax.fori_loop(1, PL // BATCH, step, 0)
        for q in range(BATCH):
            block_edges(PL - BATCH + q, (PL // BATCH - 1) % 2 * BATCH + q)
    for p in range(PL):
        for k in range(len(VARIABLE_GROUPS)):
            store_tend(k, p).wait()
        store_edges(p).wait()
    for v in range(V):
        store_patched(v).wait()
    store_early.wait()


def stencil(target, left_eig, received, flow, wave, edge_rows, early):
    return pl.pallas_call(
        stencil_kernel,
        in_specs=[OUTSIDE, OUTSIDE, RESIDENT, OUTSIDE, RESIDENT, RESIDENT, OUTSIDE],
        out_specs=[OUTSIDE] * 3,
        out_shape=[
            pltpu.HBM((V, PL, N, N), F32),
            pltpu.HBM((V, PL, N, N), F32),
            pltpu.HBM((PL, V, 2, 8, N), F32),
        ],
        scratch_shapes=[
            pltpu.SMEM((8, 32), jnp.int32),
            pltpu.SMEM((V, V), F32),
            pltpu.VMEM((V, PL, PAD, N), F32),
            pltpu.VMEM((V, PL, N, N), F32),
            pltpu.VMEM((2 * BATCH, V, N, 2 * N), BF16),
            pltpu.VMEM((V, 24, N), F32),
            pltpu.VMEM((PL, 24, N), F32),
            pltpu.VMEM((PL, V, 8, N), F32),
            pltpu.SemaphoreType.DMA((2,)),
            pltpu.SemaphoreType.DMA((V,)),
            pltpu.SemaphoreType.DMA((len(VARIABLE_GROUPS), PL)),
            pltpu.SemaphoreType.DMA((V,)),
            pltpu.SemaphoreType.DMA((PL,)),
            pltpu.SemaphoreType.DMA((1,)),
        ],
        compiler_params=room(32),
        cost_estimate=pl.CostEstimate(
            flops=10**8, bytes_accessed=18 * 10**6, transcendentals=0
        ),
        name="stencil",
    )(target, left_eig, received, in_hbm(flow), wave, edge_rows, early)


def uncoupled_kernel(
    left_eig, right_eig, both_in, tend_in, patched_in, out, both_parts, tend, base, sem, store_sem
):
    def loads(g):
        planes = pl.ds(g * PAIR, PAIR)
        return [
            pltpu.make_async_copy(source.at[:, planes], held.at[:, planes], sem.at[k, g])
            for k, (source, held) in enumerate(
                ((both_in, both_parts), (tend_in, tend), (patched_in, base))
            )
        ]

    def store(g):
        planes = pl.ds(g * PAIR, PAIR)
        return pltpu.make_async_copy(base.at[:, planes], out.at[:, planes], store_sem.at[g])

    for g in range(AHEAD):
        for copy in loads(g):
            copy.start()

    def group(g, _):
        @pl.when(g + AHEAD < GROUPS)
        def _():
            for copy in loads(g + AHEAD):
                copy.start()

        for copy in loads(g):
            copy.wait()
        for q in range(PAIR):
            p = g * PAIR + q
            solved = []
            for v in range(V):
                total = left_eig[v, 0] * tend[0, p]
                for u in range(1, V):
                    total = total + left_eig[v, u] * tend[u, p]
                solved.append(product(both_parts[v, p], split(total)))
            for u in range(V):
                total = base[u, p]
                for v in range(V):
                    total = total + right_eig[u, v] * solved[v]
                base[u, p] = total
        store(g).start()
        return 0

    lax.fori_loop(0, GROUPS, group, 0)
    for g in range(GROUPS):
        store(g).wait()


def uncoupled(left_eig, right_eig, both_parts, tend, patched):
    return pl.pallas_call(
        uncoupled_kernel,
        in_specs=[SCALARS, SCALARS, OUTSIDE, OUTSIDE, OUTSIDE],
        out_specs=OUTSIDE,
        out_shape=pltpu.HBM((V, PL, N, N), F32),
        scratch_shapes=[
            pltpu.VMEM((V, PL, N, 2 * N), BF16),
            pltpu.VMEM((V, PL, N, N), F32),
            pltpu.VMEM((V, PL, N, N), F32),
            pltpu.SemaphoreType.DMA((3, GROUPS)),
            pltpu.SemaphoreType.DMA((GROUPS,)),
        ],
        compiler_params=room(32),
        cost_estimate=pl.CostEstimate(
            flops=2 * 10**9, bytes_accessed=21 * 10**6, transcendentals=0
        ),
        name="uncoupled",
    )(left_eig, right_eig, in_hbm(both_parts), in_hbm(tend), in_hbm(patched))


def sweep_kernel(blocks, left_eig, got, out):
    take = lambda l, j: got[l, pl.ds(j, V, stride=ROWS), :]
    zero = jnp.zeros((V, N), F32)
    eig = [jnp.broadcast_to(left_eig[:, u : u + 1], (V, N)) for u in range(V)]

    def mixed(tendency):
        total = eig[0] * tendency[0:1]
        for u in range(1, V):
            total = total + eig[u] * tendency[u : u + 1]
        return total

    first, second = zero, zero
    offsets = []
    factor_up = []
    for l in range(blocks):
        speed = {e: -0.0625 * got[l, ROWS * i + 14 : ROWS * i + 15, :] for i, e in enumerate(EDGES)}
        packed = take(l, 15)
        scalar = lambda k: packed[:, k : k + 1]
        edge = {e: zero for e in EDGES}
        if l > 0:
            far, near = take(l - 1, 4), take(l - 1, 5)
            edge[0] = mixed(speed[0] * (far - 12.0 * near))
            edge[1] = mixed(speed[1] * near)
        if l < blocks - 1:
            near, far = take(l + 1, 6), take(l + 1, 7)
            edge[126] = mixed(speed[126] * near)
            edge[127] = mixed(speed[127] * (far + 4.0 * near))
        edge[0] = edge[0] - (take(l, 8) * first + take(l, 9) * second)
        edge[1] = edge[1] - take(l, 10) * first
        for i, e in enumerate(EDGES):
            out[l, pl.ds(i, V, stride=4), :] = edge[e]
        found = []
        for j in range(4):
            total = take(l, j)
            for i, e in enumerate(EDGES):
                total = total + scalar(4 * j + i) * edge[e]
            found.append(total)
        offsets.append(found[:2])
        first, second = found[3], found[2]
    first, second = zero, zero
    for l in range(blocks - 1, -1, -1):
        packed = take(l, 15)
        last = -(take(l, 11) * first + take(l, 12) * second)
        before = -(take(l, 13) * first)
        out[l, pl.ds(20, V, stride=2), :] = before
        out[l, pl.ds(21, V, stride=2), :] = last
        out[l, 30:32, :] = jnp.zeros((2, N), F32)
        first, second = [
            offsets[l][j] + packed[:, 16 + 2 * j : 17 + 2 * j] * before
            + packed[:, 17 + 2 * j : 18 + 2 * j] * last
            for j in range(2)
        ]


def sweeps(left_eig, got):
    blocks = got.shape[0]
    return pl.pallas_call(
        functools.partial(sweep_kernel, blocks),
        in_specs=[RESIDENT, RESIDENT],
        out_specs=RESIDENT,
        out_shape=jax.ShapeDtypeStruct((blocks, 32, N), F32),
        cost_estimate=pl.CostEstimate(
            flops=2 * 10**9, bytes_accessed=30 * 10**6, transcendentals=0
        ),
        compiler_params=room(32),
        name="sweeps",
    )(left_eig, got)


def coupled_kernel(pattern, base, columns, incoming, out, held, sem):
    def store(g):
        planes = pl.ds(g * PAIR, PAIR)
        return pltpu.make_async_copy(held.at[:, planes], out.at[:, planes], sem.at[g])

    def group(g, _):
        for q in range(PAIR):
            p = g * PAIR + q
            sides = []
            for u in range(V):
                scaled = incoming[p] * pattern[u]
                high = scaled.astype(BF16)
                low = (scaled - high.astype(F32)).astype(BF16)
                sides.append(jnp.concatenate([high, high, low, low], axis=0))
            change = jnp.dot(columns[p], jnp.concatenate(sides, axis=1), preferred_element_type=F32)
            for u in range(V):
                held[u, p] = base[u, p] + change[:, u * N : (u + 1) * N]
        store(g).start()
        return 0

    lax.fori_loop(0, GROUPS, group, 0)
    for g in range(GROUPS):
        store(g).wait()


def coupled(pattern, base, columns, incoming):
    return pl.pallas_call(
        coupled_kernel,
        in_specs=[RESIDENT] * 4,
        out_specs=OUTSIDE,
        out_shape=pltpu.HBM((V, PL, N, N), F32),
        scratch_shapes=[
            pltpu.VMEM((V, PL, N, N), F32),
            pltpu.SemaphoreType.DMA((GROUPS,)),
        ],
        compiler_params=room(32),
        name="coupled",
    )(pattern, base, columns, incoming)


def local(
    flow_state,
    wave_speed,
    left_eig,
    right_eig,
    lower_inverse,
    upper_inverse,
    lower_link,
    upper_link,
    donor_rows,
    stencil_offsets,
    donor_weights,
    block_counts,
    receptor_rows,
):
    flat = flow_state.reshape(V, PL * N, N)
    outgoing = gather_donors(donor_rows, stencil_offsets, donor_weights, flat)
    received = lax.all_to_all(outgoing, "plane", 0, 0, tiled=True)
    rows = receptor_rows.reshape(8, 32)
    valid = jnp.arange(32, dtype=jnp.int32)[None, :] < block_counts.reshape(8, 1)
    target = jnp.where(valid, (rows // N) * PAD + rows % N + 8, SPARE)
    lower_inverse, outgoing = lax.optimization_barrier((lower_inverse, outgoing))
    both_parts, edge_rows, columns, early, pattern = factors(
        lower_inverse,
        upper_inverse,
        wave_speed,
        lower_link.reshape(3, V, PL, N),
        upper_link.reshape(3, V, PL, N),
        right_eig,
    )
    tend, patched, edges = stencil(
        target,
        left_eig,
        received,
        flow_state,
        wave_speed,
        edge_rows,
        early,
    )
    edges = edges.reshape(PL, V * ROWS, N)
    got = lax.all_to_all(edges, "line", 0, 0, tiled=True)
    base = uncoupled(left_eig, right_eig, both_parts, tend, patched)
    got, base = lax.optimization_barrier((got, base))
    incoming = lax.all_to_all(sweeps(left_eig, got), "line", 0, 0, tiled=True)
    return coupled(pattern, base, columns, incoming)


def solution(mesh):
    in_specs = (
        P(None, "plane", "line", None),
        P("plane", "line", None),
        P(),
        P(),
        P(None, "plane", "line", None),
        P(None, "plane", "line", None),
        P(None, None, "plane", "line", None),
        P(None, None, "plane", "line", None),
        P("plane", "line", None, None),
        P("plane", "line", None, None),
        P(None, "plane", "line", None, None),
        P(None, "line", "plane"),
        P("plane", "line", None, None),
    )
    out_specs = P(None, "plane", "line", None)
    return jax.shard_map(local, mesh=mesh, in_specs=in_specs, out_specs=out_specs, check_vma=False)
```

```python
import functools

import jax
import jax.numpy as jnp
from jax import lax
from jax.experimental import pallas as pl
from jax.experimental.pallas import tpu as pltpu
from jax.sharding import PartitionSpec as P

F32 = jnp.float32
BF16 = jnp.bfloat16
V = 5
PL = 16
N = 128
PAD = 144
SPARE = 143
ROWS = 16
EDGES = (126, 127, 0, 1)
PAIR = 2
GROUPS = PL // PAIR
VARIABLE_GROUPS = ((0, 1), (2, 3, 4))
BATCH = 4
AHEAD = 3
SCALARS = pl.BlockSpec(memory_space=pltpu.SMEM)
RESIDENT = pl.BlockSpec(memory_space=pltpu.VMEM)
OUTSIDE = pl.BlockSpec(memory_space=pl.ANY)


def room(mebibytes):
    return pltpu.CompilerParams(vmem_limit_bytes=mebibytes * 2**20)


def in_hbm(x):
    return pltpu.with_memory_space_constraint(x, pltpu.HBM)


def split(x):
    high = x.astype(BF16)
    low = (x - high.astype(F32)).astype(BF16)
    return jnp.concatenate([high, low], axis=1)


def product(left_parts, right_parts):
    both = jnp.concatenate([right_parts, right_parts], axis=0)
    wide = jnp.dot(left_parts, both, preferred_element_type=F32)
    return wide[:, :N] + wide[:, N:]


def gather_kernel(
    rows_in, offsets_in, weights_in, flow, out,
    rows, offsets, weights, held, found, scalar_sem, sem, store_sem,
):
    groups = ((0, 1), (2, 3, 4))
    scalars = [
        pltpu.make_async_copy(source, to, scalar_sem.at[i])
        for i, (source, to) in enumerate(
            ((rows_in, rows), (offsets_in, offsets), (weights_in, weights))
        )
    ]
    for copy in scalars:
        copy.start()

    def load(v):
        return pltpu.make_async_copy(flow.at[v], held.at[v, pl.ds(0, PL * N)], sem.at[v])

    def store(d, k):
        part = pl.ds(groups[k][0], len(groups[k]))
        return pltpu.make_async_copy(found.at[d, part], out.at[d, part], store_sem.at[k, d])

    for v in range(V):
        load(v).start()
    for copy in scalars:
        copy.wait()
    for k, group in enumerate(groups):
        for v in group:
            load(v).wait()

        def peer(d, _):
            for c in range(32):
                first = rows[0, 0, d, c]
                second = first + offsets[0, 0, d, c]
                near, far = weights[0, 0, 0, d, c], weights[1, 0, 0, d, c]
                for v in group:
                    found[d, v, pl.ds(c, 1), :] = (
                        near * held[v, pl.ds(first, 1), :] + far * held[v, pl.ds(second, 1), :]
                    )
            store(d, k).start()
            return 0

        lax.fori_loop(0, 8, peer, 0)
    for k in range(2):
        for d in range(8):
            store(d, k).wait()


def gather_donors(donor_rows, stencil_offsets, donor_weights, flat):
    return pl.pallas_call(
        gather_kernel,
        in_specs=[OUTSIDE] * 4,
        out_specs=OUTSIDE,
        out_shape=pltpu.HBM((8, V, 32, N), F32),
        scratch_shapes=[
            pltpu.SMEM((1, 1, 8, 32), jnp.int32),
            pltpu.SMEM((1, 1, 8, 32), jnp.int32),
            pltpu.SMEM((2, 1, 1, 8, 32), F32),
            pltpu.VMEM((V, PL * N + 8, N), F32),
            pltpu.VMEM((8, V, 32, N), F32),
            pltpu.SemaphoreType.DMA((3,)),
            pltpu.SemaphoreType.DMA((V,)),
            pltpu.SemaphoreType.DMA((2, 8)),
        ],
        compiler_params=room(56),
        cost_estimate=pl.CostEstimate(flops=10**6, bytes_accessed=6 * 10**6, transcendentals=0),
        name="gather_donors",
    )(donor_rows, stencil_offsets, donor_weights, in_hbm(flat))


def factors_kernel(
    lower, upper, wave, lower_link, upper_link, right_eig,
    both_out, edge_rows, columns, early, pattern,
    lows, ups, both_parts, load_sem, store_sem,
):
    def loads(g):
        planes = pl.ds(g * PAIR, PAIR)
        return [
            pltpu.make_async_copy(source.at[:, planes], held.at[:, planes], load_sem.at[k, g])
            for k, (source, held) in enumerate(((lower, lows), (upper, ups)))
        ]

    def store(g):
        planes = pl.ds(g * PAIR, PAIR)
        return pltpu.make_async_copy(
            both_parts.at[:, planes], both_out.at[:, planes], store_sem.at[g]
        )

    for g in range(AHEAD):
        for copy in loads(g):
            copy.start()
    for u in range(V):
        for v in range(V):
            pattern[u, 4 * v : 4 * v + 4, :] = jnp.full((4, N), right_eig[u, v])
            pattern[u, 20 + 2 * v : 22 + 2 * v, :] = jnp.full((2, N), right_eig[u, v])
        pattern[u, 30:32, :] = jnp.zeros((2, N), F32)
    lane = lax.broadcasted_iota(jnp.int32, (N, N), 1)
    lane_row = lax.broadcasted_iota(jnp.int32, (1, N), 1)

    def group(g, _):
        @pl.when(g + AHEAD < GROUPS)
        def _():
            for copy in loads(g + AHEAD):
                copy.start()

        for copy in loads(g):
            copy.wait()
        for q in range(PAIR):
            p = g * PAIR + q
            cols = jnp.zeros((N, N), F32)
            ends = []
            for v in range(V):
                low, up = lows[v, p], ups[v, p]
                both = product(split(up), split(low))
                both_parts[v, p] = split(both)
                ends += [both[0:2], low[126:128]]
                at = 4 * v
                cols = jnp.where((lane >= at) & (lane < at + 4), pltpu.roll(both, at + 2, axis=1), cols)
                at = 20 + 2 * v
                cols = jnp.where((lane >= at) & (lane < at + 2), pltpu.roll(up, at + 2, axis=1), cols)
                packed = jnp.zeros((1, N), F32)
                for i, row in enumerate((both[0:1], both[1:2], low[126:127], low[127:128])):
                    at = 4 * i
                    packed = jnp.where(
                        (lane_row >= at) & (lane_row < at + 4), pltpu.roll(row, at + 2, axis=1), packed
                    )
                for i, row in enumerate((up[0:1], up[1:2])):
                    at = 16 + 2 * i
                    packed = jnp.where(
                        (lane_row >= at) & (lane_row < at + 2), pltpu.roll(row, at + 2, axis=1), packed
                    )
                for i in range(3):
                    early[p, v, i : i + 1, :] = lower_link[i, v, pl.ds(p, 1), :]
                    early[p, v, 3 + i : 4 + i, :] = upper_link[i, v, pl.ds(p, 1), :]
                point = EDGES[min(v, 3)]
                early[p, v, 6:7, :] = wave[p, point : point + 1, :]
                early[p, v, 7:8, :] = packed
            ends = jnp.concatenate(ends + [jnp.zeros((4, N), F32)], axis=0)
            high = ends.astype(BF16).astype(F32)
            edge_rows[p] = jnp.concatenate([high, ends - high], axis=0).astype(BF16)
            high = cols.astype(BF16).astype(F32)
            pair = high + pltpu.roll(cols - high, 32, axis=1)
            columns[p] = (pair + pltpu.roll(pair, 64, axis=1)).astype(BF16)
        store(g).start()
        return 0

    lax.fori_loop(0, GROUPS, group, 0)
    for g in range(GROUPS):
        store(g).wait()


def factors(lower_inverse, upper_inverse, wave, lower_link, upper_link, right_eig):
    return pl.pallas_call(
        factors_kernel,
        in_specs=[OUTSIDE] * 2 + [RESIDENT] * 3 + [SCALARS],
        out_specs=[OUTSIDE] + [RESIDENT] * 4,
        out_shape=[
            pltpu.HBM((V, PL, N, 2 * N), BF16),
            jax.ShapeDtypeStruct((PL, 48, N), BF16),
            pltpu.HBM((PL, N, N), BF16),
            jax.ShapeDtypeStruct((PL, V, 8, N), F32),
            pltpu.HBM((V, 32, N), F32),
        ],
        scratch_shapes=[
            pltpu.VMEM((V, PL, N, N), F32),
            pltpu.VMEM((V, PL, N, N), F32),
            pltpu.VMEM((V, PL, N, 2 * N), BF16),
            pltpu.SemaphoreType.DMA((2, GROUPS)),
            pltpu.SemaphoreType.DMA((GROUPS,)),
        ],
        compiler_params=room(32),
        cost_estimate=pl.CostEstimate(
            flops=2 * 10**9, bytes_accessed=17 * 10**6, transcendentals=0
        ),
        name="factors",
    )(
        in_hbm(lower_inverse), in_hbm(upper_inverse), wave, lower_link, upper_link, right_eig
    )


def stencil_kernel(
    target_in, eig_in, received, flow, wave, edge_rows, early,
    tend_out, patched, edges_out,
    target, left_eig, grid_rows, tend, parts, pattern, sums, edges,
    scalar_sem, load_sem, tend_sem, patch_sem, edge_sem, early_sem,
):
    def load(v):
        return pltpu.make_async_copy(flow.at[v], grid_rows.at[v, :, pl.ds(8, N), :], load_sem.at[v])

    def store_tend(k, p):
        part = pl.ds(VARIABLE_GROUPS[k][0], len(VARIABLE_GROUPS[k]))
        return pltpu.make_async_copy(tend.at[part, p], tend_out.at[part, p], tend_sem.at[k, p])

    def store_edges(p):
        return pltpu.make_async_copy(edges.at[p], edges_out.at[p, :, 0], edge_sem.at[p])

    def store_patched(v):
        return pltpu.make_async_copy(
            grid_rows.at[v, :, pl.ds(8, N), :], patched.at[v], patch_sem.at[v]
        )

    copies = [
        pltpu.make_async_copy(target_in, target, scalar_sem.at[0]),
        pltpu.make_async_copy(eig_in, left_eig, scalar_sem.at[1]),
    ]
    for copy in copies:
        copy.start()
    for v in range(V):
        load(v).start()
    store_early = pltpu.make_async_copy(early, edges_out.at[:, :, 1], early_sem.at[0])
    store_early.start()
    flat_rows = grid_rows.reshape(V, PL * PAD, N)
    zeros = jnp.zeros((8, N), F32)
    for v in range(V):
        for q in range(PL):
            grid_rows[v, q, 0:8, :] = zeros
            grid_rows[v, q, 136:144, :] = zeros
    for copy in copies:
        copy.wait()
    for u in range(V):
        for v in range(V):
            pattern[u, 4 * v : 4 * v + 4, :] = jnp.full((4, N), left_eig[v, u])
        pattern[u, 20:24, :] = jnp.zeros((4, N), F32)
    lane = lax.broadcasted_iota(jnp.int32, (32, N), 1)

    for k, group in enumerate(VARIABLE_GROUPS):
        first, last = k == 0, k == len(VARIABLE_GROUPS) - 1
        for v in group:
            load(v).wait()

        def place(d, _):
            for c in range(32):
                row = target[d, c]
                for v in group:
                    flat_rows[v, pl.ds(row, 1), :] = received[d, v, pl.ds(c, 1), :]
            return 0

        lax.fori_loop(0, 8, place, 0)
        for v in group:
            store_patched(v).start()

        def tendency(p, slot):
            for start in range(0, N, 32):
                speed = -0.0625 * wave[p, pl.ds(start, 32), :]
                for v in group:
                    at = lambda shift: grid_rows[v, p, pl.ds(8 + start + shift, 32), :]
                    here = at(0)
                    after = jnp.where(lane == N - 1, 0.0, pltpu.roll(here, N - 1, axis=1))
                    before = jnp.where(lane == 0, 0.0, pltpu.roll(here, 1, axis=1))
                    near = (at(1) - 3.0 * at(-1)) + (1.5 * here + 2.0 * (after - before))
                    total = speed * ((at(2) + at(-2)) + 4.0 * near)
                    tend[v, p, pl.ds(start, 32), :] = total
                    parts[slot, v, pl.ds(start, 32), :] = split(total)
            store_tend(k, p).start()

        def block_edges(p, slot):
            total = jnp.zeros((24, N), F32) if first else sums[p]
            for u in group:
                wide = jnp.dot(
                    edge_rows[p], parts[slot, u], preferred_element_type=F32
                )
                found = wide[:, :N] + wide[:, N:]
                total = total + pattern[u] * (found[:24] + found[24:])
            if not last:
                sums[p] = total
            for v in group:
                edges[p, v, 4:6, :] = grid_rows[v, p, 134:136, :]
                edges[p, v, 6:8, :] = grid_rows[v, p, 8:10, :]
            if last:
                for v in range(V):
                    edges[p, v, 0:4, :] = total[4 * v : 4 * v + 4]
                store_edges(p).start()

        def step(i, _):
            before, now = lax.rem(i + 1, 2) * BATCH, lax.rem(i, 2) * BATCH
            for q in range(BATCH):
                block_edges((i - 1) * BATCH + q, before + q)
            for q in range(BATCH):
                tendency(i * BATCH + q, now + q)
            return 0

        for q in range(BATCH):
            tendency(q, q)
        lax.fori_loop(1, PL // BATCH, step, 0)
        for q in range(BATCH):
            block_edges(PL - BATCH + q, (PL // BATCH - 1) % 2 * BATCH + q)
    for p in range(PL):
        for k in range(len(VARIABLE_GROUPS)):
            store_tend(k, p).wait()
        store_edges(p).wait()
    for v in range(V):
        store_patched(v).wait()
    store_early.wait()


def stencil(target, left_eig, received, flow, wave, edge_rows, early):
    return pl.pallas_call(
        stencil_kernel,
        in_specs=[OUTSIDE, OUTSIDE, RESIDENT, OUTSIDE, RESIDENT, RESIDENT, OUTSIDE],
        out_specs=[OUTSIDE] * 3,
        out_shape=[
            pltpu.HBM((V, PL, N, N), F32),
            pltpu.HBM((V, PL, N, N), F32),
            pltpu.HBM((PL, V, 2, 8, N), F32),
        ],
        scratch_shapes=[
            pltpu.SMEM((8, 32), jnp.int32),
            pltpu.SMEM((V, V), F32),
            pltpu.VMEM((V, PL, PAD, N), F32),
            pltpu.VMEM((V, PL, N, N), F32),
            pltpu.VMEM((2 * BATCH, V, N, 2 * N), BF16),
            pltpu.VMEM((V, 24, N), F32),
            pltpu.VMEM((PL, 24, N), F32),
            pltpu.VMEM((PL, V, 8, N), F32),
            pltpu.SemaphoreType.DMA((2,)),
            pltpu.SemaphoreType.DMA((V,)),
            pltpu.SemaphoreType.DMA((len(VARIABLE_GROUPS), PL)),
            pltpu.SemaphoreType.DMA((V,)),
            pltpu.SemaphoreType.DMA((PL,)),
            pltpu.SemaphoreType.DMA((1,)),
        ],
        compiler_params=room(32),
        cost_estimate=pl.CostEstimate(
            flops=10**8, bytes_accessed=18 * 10**6, transcendentals=0
        ),
        name="stencil",
    )(target, left_eig, received, in_hbm(flow), wave, edge_rows, early)


def uncoupled_kernel(
    left_eig, right_eig, both_in, tend_in, patched_in, out, both_parts, tend, base, sem, store_sem
):
    def loads(g):
        planes = pl.ds(g * PAIR, PAIR)
        return [
            pltpu.make_async_copy(source.at[:, planes], held.at[:, planes], sem.at[k, g])
            for k, (source, held) in enumerate(
                ((both_in, both_parts), (tend_in, tend), (patched_in, base))
            )
        ]

    def store(g):
        planes = pl.ds(g * PAIR, PAIR)
        return pltpu.make_async_copy(base.at[:, planes], out.at[:, planes], store_sem.at[g])

    for g in range(AHEAD):
        for copy in loads(g):
            copy.start()

    def group(g, _):
        @pl.when(g + AHEAD < GROUPS)
        def _():
            for copy in loads(g + AHEAD):
                copy.start()

        for copy in loads(g):
            copy.wait()
        for q in range(PAIR):
            p = g * PAIR + q
            solved = []
            for v in range(V):
                total = left_eig[v, 0] * tend[0, p]
                for u in range(1, V):
                    total = total + left_eig[v, u] * tend[u, p]
                solved.append(product(both_parts[v, p], split(total)))
            for u in range(V):
                total = base[u, p]
                for v in range(V):
                    total = total + right_eig[u, v] * solved[v]
                base[u, p] = total
        store(g).start()
        return 0

    lax.fori_loop(0, GROUPS, group, 0)
    for g in range(GROUPS):
        store(g).wait()


def uncoupled(left_eig, right_eig, both_parts, tend, patched):
    return pl.pallas_call(
        uncoupled_kernel,
        in_specs=[SCALARS, SCALARS, OUTSIDE, OUTSIDE, OUTSIDE],
        out_specs=OUTSIDE,
        out_shape=pltpu.HBM((V, PL, N, N), F32),
        scratch_shapes=[
            pltpu.VMEM((V, PL, N, 2 * N), BF16),
            pltpu.VMEM((V, PL, N, N), F32),
            pltpu.VMEM((V, PL, N, N), F32),
            pltpu.SemaphoreType.DMA((3, GROUPS)),
            pltpu.SemaphoreType.DMA((GROUPS,)),
        ],
        compiler_params=room(32),
        cost_estimate=pl.CostEstimate(
            flops=2 * 10**9, bytes_accessed=21 * 10**6, transcendentals=0
        ),
        name="uncoupled",
    )(left_eig, right_eig, in_hbm(both_parts), in_hbm(tend), in_hbm(patched))


def sweep_kernel(blocks, left_eig, got, out, rows, found_rows):
    height = V * ROWS
    for l in range(blocks):
        rows[l * height : (l + 1) * height, :] = got[l]
    take = lambda l, j: rows[pl.ds(l * height + j, V, stride=ROWS), :]
    zero = jnp.zeros((V, N), F32)
    eig = [jnp.broadcast_to(left_eig[:, u : u + 1], (V, N)) for u in range(V)]

    def mixed(tendency):
        total = eig[0] * tendency[0:1]
        for u in range(1, V):
            total = total + eig[u] * tendency[u : u + 1]
        return total

    first, second = zero, zero
    offsets = []
    for l in range(blocks):
        speed = {
            e: -0.0625 * got[l, ROWS * i + 14 : ROWS * i + 15, :] for i, e in enumerate(EDGES)
        }
        packed = take(l, 15)
        scalar = lambda k: packed[:, k : k + 1]
        edge = {e: zero for e in EDGES}
        if l > 0:
            far, near = take(l - 1, 4), take(l - 1, 5)
            edge[0] = mixed(speed[0] * (far - 12.0 * near))
            edge[1] = mixed(speed[1] * near)
        if l < blocks - 1:
            near, far = take(l + 1, 6), take(l + 1, 7)
            edge[126] = mixed(speed[126] * near)
            edge[127] = mixed(speed[127] * (far + 4.0 * near))
        edge[0] = edge[0] - (take(l, 8) * first + take(l, 9) * second)
        edge[1] = edge[1] - take(l, 10) * first
        for i, e in enumerate(EDGES):
            found_rows[pl.ds(32 * l + i, V, stride=4), :] = edge[e]
        found = []
        for j in range(4):
            total = take(l, j)
            for i, e in enumerate(EDGES):
                total = total + scalar(4 * j + i) * edge[e]
            found.append(total)
        offsets.append(found[:2])
        first, second = found[3], found[2]
    first, second = zero, zero
    for l in range(blocks - 1, -1, -1):
        packed = take(l, 15)
        last = -(take(l, 11) * first + take(l, 12) * second)
        before = -(take(l, 13) * first)
        found_rows[pl.ds(32 * l + 20, V, stride=2), :] = before
        found_rows[pl.ds(32 * l + 21, V, stride=2), :] = last
        found_rows[32 * l + 30 : 32 * l + 32, :] = jnp.zeros((2, N), F32)
        out[l] = found_rows[32 * l : 32 * l + 32, :]
        first, second = [
            offsets[l][j] + packed[:, 16 + 2 * j : 17 + 2 * j] * before
            + packed[:, 17 + 2 * j : 18 + 2 * j] * last
            for j in range(2)
        ]


def sweeps(left_eig, got):
    blocks = got.shape[0]
    return pl.pallas_call(
        functools.partial(sweep_kernel, blocks),
        in_specs=[RESIDENT, RESIDENT],
        out_specs=RESIDENT,
        out_shape=jax.ShapeDtypeStruct((blocks, 32, N), F32),
        scratch_shapes=[
            pltpu.VMEM((blocks * V * ROWS + 8 * ROWS, N), F32),
            pltpu.VMEM((blocks * 32 + 64, N), F32),
        ],
        cost_estimate=pl.CostEstimate(
            flops=2 * 10**9, bytes_accessed=30 * 10**6, transcendentals=0
        ),
        compiler_params=room(32),
        name="sweeps",
    )(left_eig, got)


def coupled_kernel(pattern, base, columns, incoming, out, held, sem):
    def store(g):
        planes = pl.ds(g * PAIR, PAIR)
        return pltpu.make_async_copy(held.at[:, planes], out.at[:, planes], sem.at[g])

    def group(g, _):
        for q in range(PAIR):
            p = g * PAIR + q
            sides = []
            for u in range(V):
                scaled = incoming[p] * pattern[u]
                high = scaled.astype(BF16)
                low = (scaled - high.astype(F32)).astype(BF16)
                sides.append(jnp.concatenate([high, high, low, low], axis=0))
            change = jnp.dot(columns[p], jnp.concatenate(sides, axis=1), preferred_element_type=F32)
            for u in range(V):
                held[u, p] = base[u, p] + change[:, u * N : (u + 1) * N]
        store(g).start()
        return 0

    lax.fori_loop(0, GROUPS, group, 0)
    for g in range(GROUPS):
        store(g).wait()


def coupled(pattern, base, columns, incoming):
    return pl.pallas_call(
        coupled_kernel,
        in_specs=[RESIDENT] * 4,
        out_specs=OUTSIDE,
        out_shape=pltpu.HBM((V, PL, N, N), F32),
        scratch_shapes=[
            pltpu.VMEM((V, PL, N, N), F32),
            pltpu.SemaphoreType.DMA((GROUPS,)),
        ],
        compiler_params=room(32),
        name="coupled",
    )(pattern, base, columns, incoming)


def local(
    flow_state,
    wave_speed,
    left_eig,
    right_eig,
    lower_inverse,
    upper_inverse,
    lower_link,
    upper_link,
    donor_rows,
    stencil_offsets,
    donor_weights,
    block_counts,
    receptor_rows,
):
    flat = flow_state.reshape(V, PL * N, N)
    outgoing = gather_donors(donor_rows, stencil_offsets, donor_weights, flat)
    received = lax.all_to_all(outgoing, "plane", 0, 0, tiled=True)
    rows = receptor_rows.reshape(8, 32)
    valid = jnp.arange(32, dtype=jnp.int32)[None, :] < block_counts.reshape(8, 1)
    target = jnp.where(valid, (rows // N) * PAD + rows % N + 8, SPARE)
    lower_inverse, outgoing = lax.optimization_barrier((lower_inverse, outgoing))
    both_parts, edge_rows, columns, early, pattern = factors(
        lower_inverse,
        upper_inverse,
        wave_speed,
        lower_link.reshape(3, V, PL, N),
        upper_link.reshape(3, V, PL, N),
        right_eig,
    )
    tend, patched, edges = stencil(
        target,
        left_eig,
        received,
        flow_state,
        wave_speed,
        edge_rows,
        early,
    )
    edges = edges.reshape(PL, V * ROWS, N)
    got = lax.all_to_all(edges, "line", 0, 0, tiled=True)
    base = uncoupled(left_eig, right_eig, both_parts, tend, patched)
    got, base = lax.optimization_barrier((got, base))
    incoming = lax.all_to_all(sweeps(left_eig, got), "line", 0, 0, tiled=True)
    return coupled(pattern, base, columns, incoming)


def solution(mesh):
    in_specs = (
        P(None, "plane", "line", None),
        P("plane", "line", None),
        P(),
        P(),
        P(None, "plane", "line", None),
        P(None, "plane", "line", None),
        P(None, None, "plane", "line", None),
        P(None, None, "plane", "line", None),
        P("plane", "line", None, None),
        P("plane", "line", None, None),
        P(None, "plane", "line", None, None),
        P(None, "line", "plane"),
        P("plane", "line", None, None),
    )
    out_specs = P(None, "plane", "line", None)
    return jax.shard_map(local, mesh=mesh, in_specs=in_specs, out_specs=out_specs, check_vma=False)
```

```python
import functools

import jax
import jax.numpy as jnp
from jax import lax
from jax.experimental import pallas as pl
from jax.experimental.pallas import tpu as pltpu
from jax.sharding import PartitionSpec as P

F32 = jnp.float32
BF16 = jnp.bfloat16
V = 5
PL = 16
N = 128
PAD = 144
SPARE = 143
ROWS = 16
EDGES = (126, 127, 0, 1)
PAIR = 2
GROUPS = PL // PAIR
LAST_PLANES = 4
LAST_GROUPS = PL // LAST_PLANES
VARIABLE_GROUPS = ((0, 1), (2, 3, 4))
BATCH = 4
AHEAD = 3
SCALARS = pl.BlockSpec(memory_space=pltpu.SMEM)
RESIDENT = pl.BlockSpec(memory_space=pltpu.VMEM)
OUTSIDE = pl.BlockSpec(memory_space=pl.ANY)


def room(mebibytes):
    return pltpu.CompilerParams(vmem_limit_bytes=mebibytes * 2**20)


def in_hbm(x):
    return pltpu.with_memory_space_constraint(x, pltpu.HBM)


def split(x):
    high = x.astype(BF16)
    low = (x - high.astype(F32)).astype(BF16)
    return jnp.concatenate([high, low], axis=1)


def product(left_parts, right_parts):
    both = jnp.concatenate([right_parts, right_parts], axis=0)
    wide = jnp.dot(left_parts, both, preferred_element_type=F32)
    return wide[:, :N] + wide[:, N:]


def gather_kernel(
    rows_in, offsets_in, weights_in, flow, out,
    rows, offsets, weights, held, found, scalar_sem, sem, store_sem,
):
    groups = ((0, 1), (2, 3, 4))
    scalars = [
        pltpu.make_async_copy(source, to, scalar_sem.at[i])
        for i, (source, to) in enumerate(
            ((rows_in, rows), (offsets_in, offsets), (weights_in, weights))
        )
    ]
    for copy in scalars:
        copy.start()

    def load(v):
        return pltpu.make_async_copy(flow.at[v], held.at[v, pl.ds(0, PL * N)], sem.at[v])

    def store(d, k):
        part = pl.ds(groups[k][0], len(groups[k]))
        return pltpu.make_async_copy(found.at[d, part], out.at[d, part], store_sem.at[k, d])

    for v in range(V):
        load(v).start()
    for copy in scalars:
        copy.wait()
    for k, group in enumerate(groups):
        for v in group:
            load(v).wait()

        def peer(d, _):
            for c in range(32):
                first = rows[0, 0, d, c]
                second = first + offsets[0, 0, d, c]
                near, far = weights[0, 0, 0, d, c], weights[1, 0, 0, d, c]
                for v in group:
                    found[d, v, pl.ds(c, 1), :] = (
                        near * held[v, pl.ds(first, 1), :] + far * held[v, pl.ds(second, 1), :]
                    )
            store(d, k).start()
            return 0

        lax.fori_loop(0, 8, peer, 0)
    for k in range(2):
        for d in range(8):
            store(d, k).wait()


def gather_donors(donor_rows, stencil_offsets, donor_weights, flat):
    return pl.pallas_call(
        gather_kernel,
        in_specs=[OUTSIDE] * 4,
        out_specs=OUTSIDE,
        out_shape=pltpu.HBM((8, V, 32, N), F32),
        scratch_shapes=[
            pltpu.SMEM((1, 1, 8, 32), jnp.int32),
            pltpu.SMEM((1, 1, 8, 32), jnp.int32),
            pltpu.SMEM((2, 1, 1, 8, 32), F32),
            pltpu.VMEM((V, PL * N + 8, N), F32),
            pltpu.VMEM((8, V, 32, N), F32),
            pltpu.SemaphoreType.DMA((3,)),
            pltpu.SemaphoreType.DMA((V,)),
            pltpu.SemaphoreType.DMA((2, 8)),
        ],
        compiler_params=room(56),
        cost_estimate=pl.CostEstimate(flops=10**6, bytes_accessed=6 * 10**6, transcendentals=0),
        name="gather_donors",
    )(donor_rows, stencil_offsets, donor_weights, in_hbm(flat))


def factors_kernel(
    lower, upper, wave, lower_link, upper_link, right_eig,
    both_out, edge_rows, columns, early, pattern,
    lows, ups, both_parts, load_sem, store_sem,
):
    def loads(g):
        planes = pl.ds(g * PAIR, PAIR)
        return [
            pltpu.make_async_copy(source.at[:, planes], held.at[:, planes], load_sem.at[k, g])
            for k, (source, held) in enumerate(((lower, lows), (upper, ups)))
        ]

    def store(g):
        planes = pl.ds(g * PAIR, PAIR)
        return pltpu.make_async_copy(
            both_parts.at[:, planes], both_out.at[:, planes], store_sem.at[g]
        )

    for g in range(AHEAD):
        for copy in loads(g):
            copy.start()
    for u in range(V):
        for v in range(V):
            pattern[u, 4 * v : 4 * v + 4, :] = jnp.full((4, N), right_eig[u, v])
            pattern[u, 20 + 2 * v : 22 + 2 * v, :] = jnp.full((2, N), right_eig[u, v])
        pattern[u, 30:32, :] = jnp.zeros((2, N), F32)
    lane = lax.broadcasted_iota(jnp.int32, (N, N), 1)
    lane_row = lax.broadcasted_iota(jnp.int32, (1, N), 1)

    def group(g, _):
        @pl.when(g + AHEAD < GROUPS)
        def _():
            for copy in loads(g + AHEAD):
                copy.start()

        for copy in loads(g):
            copy.wait()
        for q in range(PAIR):
            p = g * PAIR + q
            cols = jnp.zeros((N, N), F32)
            ends = []
            for v in range(V):
                low, up = lows[v, p], ups[v, p]
                both = product(split(up), split(low))
                both_parts[v, p] = split(both)
                ends += [both[0:2], low[126:128]]
                at = 4 * v
                cols = jnp.where((lane >= at) & (lane < at + 4), pltpu.roll(both, at + 2, axis=1), cols)
                at = 20 + 2 * v
                cols = jnp.where((lane >= at) & (lane < at + 2), pltpu.roll(up, at + 2, axis=1), cols)
                packed = jnp.zeros((1, N), F32)
                for i, row in enumerate((both[0:1], both[1:2], low[126:127], low[127:128])):
                    at = 4 * i
                    packed = jnp.where(
                        (lane_row >= at) & (lane_row < at + 4), pltpu.roll(row, at + 2, axis=1), packed
                    )
                for i, row in enumerate((up[0:1], up[1:2])):
                    at = 16 + 2 * i
                    packed = jnp.where(
                        (lane_row >= at) & (lane_row < at + 2), pltpu.roll(row, at + 2, axis=1), packed
                    )
                for i in range(3):
                    early[p, v, i : i + 1, :] = lower_link[i, v, pl.ds(p, 1), :]
                    early[p, v, 3 + i : 4 + i, :] = upper_link[i, v, pl.ds(p, 1), :]
                point = EDGES[min(v, 3)]
                early[p, v, 6:7, :] = wave[p, point : point + 1, :]
                early[p, v, 7:8, :] = packed
            ends = jnp.concatenate(ends + [jnp.zeros((4, N), F32)], axis=0)
            high = ends.astype(BF16).astype(F32)
            edge_rows[p] = jnp.concatenate([high, ends - high], axis=0).astype(BF16)
            high = cols.astype(BF16).astype(F32)
            pair = high + pltpu.roll(cols - high, 32, axis=1)
            columns[p] = (pair + pltpu.roll(pair, 64, axis=1)).astype(BF16)
        store(g).start()
        return 0

    lax.fori_loop(0, GROUPS, group, 0)
    for g in range(GROUPS):
        store(g).wait()


def factors(lower_inverse, upper_inverse, wave, lower_link, upper_link, right_eig):
    return pl.pallas_call(
        factors_kernel,
        in_specs=[OUTSIDE] * 2 + [RESIDENT] * 3 + [SCALARS],
        out_specs=[OUTSIDE] + [RESIDENT] * 4,
        out_shape=[
            pltpu.HBM((V, PL, N, 2 * N), BF16),
            jax.ShapeDtypeStruct((PL, 48, N), BF16),
            pltpu.HBM((PL, N, N), BF16),
            jax.ShapeDtypeStruct((PL, V, 8, N), F32),
            pltpu.HBM((V, 32, N), F32),
        ],
        scratch_shapes=[
            pltpu.VMEM((V, PL, N, N), F32),
            pltpu.VMEM((V, PL, N, N), F32),
            pltpu.VMEM((V, PL, N, 2 * N), BF16),
            pltpu.SemaphoreType.DMA((2, GROUPS)),
            pltpu.SemaphoreType.DMA((GROUPS,)),
        ],
        compiler_params=room(32),
        cost_estimate=pl.CostEstimate(
            flops=2 * 10**9, bytes_accessed=17 * 10**6, transcendentals=0
        ),
        name="factors",
    )(
        in_hbm(lower_inverse), in_hbm(upper_inverse), wave, lower_link, upper_link, right_eig
    )


def stencil_kernel(
    target_in, eig_in, received, flow, wave, edge_rows, early,
    tend_out, patched, edges_out,
    target, left_eig, grid_rows, tend, parts, pattern, sums, edges,
    scalar_sem, load_sem, tend_sem, patch_sem, edge_sem, early_sem,
):
    def load(v):
        return pltpu.make_async_copy(flow.at[v], grid_rows.at[v, :, pl.ds(8, N), :], load_sem.at[v])

    def store_tend(k, p):
        part = pl.ds(VARIABLE_GROUPS[k][0], len(VARIABLE_GROUPS[k]))
        return pltpu.make_async_copy(tend.at[part, p], tend_out.at[part, p], tend_sem.at[k, p])

    def store_edges(p):
        return pltpu.make_async_copy(edges.at[p], edges_out.at[p, :, 0], edge_sem.at[p])

    def store_patched(v):
        return pltpu.make_async_copy(
            grid_rows.at[v, :, pl.ds(8, N), :], patched.at[v], patch_sem.at[v]
        )

    copies = [
        pltpu.make_async_copy(target_in, target, scalar_sem.at[0]),
        pltpu.make_async_copy(eig_in, left_eig, scalar_sem.at[1]),
    ]
    for copy in copies:
        copy.start()
    for v in range(V):
        load(v).start()
    store_early = pltpu.make_async_copy(early, edges_out.at[:, :, 1], early_sem.at[0])
    store_early.start()
    flat_rows = grid_rows.reshape(V, PL * PAD, N)
    zeros = jnp.zeros((8, N), F32)
    for v in range(V):
        for q in range(PL):
            grid_rows[v, q, 0:8, :] = zeros
            grid_rows[v, q, 136:144, :] = zeros
    for copy in copies:
        copy.wait()
    for u in range(V):
        for v in range(V):
            pattern[u, 4 * v : 4 * v + 4, :] = jnp.full((4, N), left_eig[v, u])
        pattern[u, 20:24, :] = jnp.zeros((4, N), F32)
    lane = lax.broadcasted_iota(jnp.int32, (16, N), 1)

    for k, group in enumerate(VARIABLE_GROUPS):
        first, last = k == 0, k == len(VARIABLE_GROUPS) - 1
        for v in group:
            load(v).wait()

        def place(d, _):
            for c in range(32):
                row = target[d, c]
                for v in group:
                    flat_rows[v, pl.ds(row, 1), :] = received[d, v, pl.ds(c, 1), :]
            return 0

        lax.fori_loop(0, 8, place, 0)
        for v in group:
            store_patched(v).start()

        def tendency(p, slot):
            for start in range(0, N, 16):
                speed = -0.0625 * wave[p, pl.ds(start, 16), :]
                for v in group:
                    at = lambda shift: grid_rows[v, p, pl.ds(8 + start + shift, 16), :]
                    here = at(0)
                    after = jnp.where(lane == N - 1, 0.0, pltpu.roll(here, N - 1, axis=1))
                    before = jnp.where(lane == 0, 0.0, pltpu.roll(here, 1, axis=1))
                    near = (at(1) - 3.0 * at(-1)) + (1.5 * here + 2.0 * (after - before))
                    total = speed * ((at(2) + at(-2)) + 4.0 * near)
                    tend[v, p, pl.ds(start, 16), :] = total
                    parts[slot, v, pl.ds(start, 16), :] = split(total)
            store_tend(k, p).start()

        def block_edges(p, slot):
            total = jnp.zeros((24, N), F32) if first else sums[p]
            for u in group:
                wide = jnp.dot(
                    edge_rows[p], parts[slot, u], preferred_element_type=F32
                )
                found = wide[:, :N] + wide[:, N:]
                total = total + pattern[u] * (found[:24] + found[24:])
            if not last:
                sums[p] = total
            for v in group:
                edges[p, v, 4:6, :] = grid_rows[v, p, 134:136, :]
                edges[p, v, 6:8, :] = grid_rows[v, p, 8:10, :]
            if last:
                for v in range(V):
                    edges[p, v, 0:4, :] = total[4 * v : 4 * v + 4]
                store_edges(p).start()

        def step(i, _):
            before, now = lax.rem(i + 1, 2) * BATCH, lax.rem(i, 2) * BATCH
            for q in range(BATCH):
                block_edges((i - 1) * BATCH + q, before + q)
            for q in range(BATCH):
                tendency(i * BATCH + q, now + q)
            return 0

        for q in range(BATCH):
            tendency(q, q)
        lax.fori_loop(1, PL // BATCH, step, 0)
        for q in range(BATCH):
            block_edges(PL - BATCH + q, (PL // BATCH - 1) % 2 * BATCH + q)
    for p in range(PL):
        for k in range(len(VARIABLE_GROUPS)):
            store_tend(k, p).wait()
        store_edges(p).wait()
    for v in range(V):
        store_patched(v).wait()
    store_early.wait()


def stencil(target, left_eig, received, flow, wave, edge_rows, early):
    return pl.pallas_call(
        stencil_kernel,
        in_specs=[OUTSIDE, OUTSIDE, RESIDENT, OUTSIDE, RESIDENT, RESIDENT, OUTSIDE],
        out_specs=[OUTSIDE] * 3,
        out_shape=[
            pltpu.HBM((V, PL, N, N), F32),
            pltpu.HBM((V, PL, N, N), F32),
            pltpu.HBM((PL, V, 2, 8, N), F32),
        ],
        scratch_shapes=[
            pltpu.SMEM((8, 32), jnp.int32),
            pltpu.SMEM((V, V), F32),
            pltpu.VMEM((V, PL, PAD, N), F32),
            pltpu.VMEM((V, PL, N, N), F32),
            pltpu.VMEM((2 * BATCH, V, N, 2 * N), BF16),
            pltpu.VMEM((V, 24, N), F32),
            pltpu.VMEM((PL, 24, N), F32),
            pltpu.VMEM((PL, V, 8, N), F32),
            pltpu.SemaphoreType.DMA((2,)),
            pltpu.SemaphoreType.DMA((V,)),
            pltpu.SemaphoreType.DMA((len(VARIABLE_GROUPS), PL)),
            pltpu.SemaphoreType.DMA((V,)),
            pltpu.SemaphoreType.DMA((PL,)),
            pltpu.SemaphoreType.DMA((1,)),
        ],
        compiler_params=room(32),
        cost_estimate=pl.CostEstimate(
            flops=10**8, bytes_accessed=18 * 10**6, transcendentals=0
        ),
        name="stencil",
    )(target, left_eig, received, in_hbm(flow), wave, edge_rows, early)


def uncoupled_kernel(
    left_eig, right_eig, both_in, tend_in, patched_in, out, both_parts, tend, base, sem, store_sem
):
    def loads(g):
        planes = pl.ds(g * PAIR, PAIR)
        return [
            pltpu.make_async_copy(source.at[:, planes], held.at[:, planes], sem.at[k, g])
            for k, (source, held) in enumerate(
                ((both_in, both_parts), (tend_in, tend), (patched_in, base))
            )
        ]

    def store(g):
        planes = pl.ds(g * PAIR, PAIR)
        return pltpu.make_async_copy(base.at[:, planes], out.at[:, planes], store_sem.at[g])

    for g in range(AHEAD):
        for copy in loads(g):
            copy.start()

    def group(g, _):
        @pl.when(g + AHEAD < GROUPS)
        def _():
            for copy in loads(g + AHEAD):
                copy.start()

        for copy in loads(g):
            copy.wait()
        for q in range(PAIR):
            p = g * PAIR + q
            solved = []
            for v in range(V):
                total = left_eig[v, 0] * tend[0, p]
                for u in range(1, V):
                    total = total + left_eig[v, u] * tend[u, p]
                solved.append(product(both_parts[v, p], split(total)))
            for u in range(V):
                total = base[u, p]
                for v in range(V):
                    total = total + right_eig[u, v] * solved[v]
                base[u, p] = total
        store(g).start()
        return 0

    lax.fori_loop(0, GROUPS, group, 0)
    for g in range(GROUPS):
        store(g).wait()


def uncoupled(left_eig, right_eig, both_parts, tend, patched):
    return pl.pallas_call(
        uncoupled_kernel,
        in_specs=[SCALARS, SCALARS, OUTSIDE, OUTSIDE, OUTSIDE],
        out_specs=OUTSIDE,
        out_shape=pltpu.HBM((V, PL, N, N), F32),
        scratch_shapes=[
            pltpu.VMEM((V, PL, N, 2 * N), BF16),
            pltpu.VMEM((V, PL, N, N), F32),
            pltpu.VMEM((V, PL, N, N), F32),
            pltpu.SemaphoreType.DMA((3, GROUPS)),
            pltpu.SemaphoreType.DMA((GROUPS,)),
        ],
        compiler_params=room(32),
        cost_estimate=pl.CostEstimate(
            flops=2 * 10**9, bytes_accessed=21 * 10**6, transcendentals=0
        ),
        name="uncoupled",
    )(left_eig, right_eig, in_hbm(both_parts), in_hbm(tend), in_hbm(patched))


def sweep_kernel(blocks, left_eig, got, out, rows, found_rows):
    height = V * ROWS
    for l in range(blocks):
        rows[l * height : (l + 1) * height, :] = got[l]
    take = lambda l, j: rows[pl.ds(l * height + j, V, stride=ROWS), :]
    zero = jnp.zeros((V, N), F32)
    eig = [jnp.broadcast_to(left_eig[:, u : u + 1], (V, N)) for u in range(V)]

    def mixed(tendency):
        total = eig[0] * tendency[0:1]
        for u in range(1, V):
            total = total + eig[u] * tendency[u : u + 1]
        return total

    first, second = zero, zero
    offsets = []
    for l in range(blocks):
        speed = {
            e: -0.0625 * got[l, ROWS * i + 14 : ROWS * i + 15, :] for i, e in enumerate(EDGES)
        }
        packed = take(l, 15)
        scalar = lambda k: packed[:, k : k + 1]
        edge = {e: zero for e in EDGES}
        if l > 0:
            far, near = take(l - 1, 4), take(l - 1, 5)
            edge[0] = mixed(speed[0] * (far - 12.0 * near))
            edge[1] = mixed(speed[1] * near)
        if l < blocks - 1:
            near, far = take(l + 1, 6), take(l + 1, 7)
            edge[126] = mixed(speed[126] * near)
            edge[127] = mixed(speed[127] * (far + 4.0 * near))
        edge[0] = edge[0] - (take(l, 8) * first + take(l, 9) * second)
        edge[1] = edge[1] - take(l, 10) * first
        for i, e in enumerate(EDGES):
            found_rows[pl.ds(32 * l + i, V, stride=4), :] = edge[e]
        found = []
        for j in range(4):
            total = take(l, j)
            for i, e in enumerate(EDGES):
                total = total + scalar(4 * j + i) * edge[e]
            found.append(total)
        offsets.append(found[:2])
        first, second = found[3], found[2]
    first, second = zero, zero
    for l in range(blocks - 1, -1, -1):
        packed = take(l, 15)
        last = -(take(l, 11) * first + take(l, 12) * second)
        before = -(take(l, 13) * first)
        found_rows[pl.ds(32 * l + 20, V, stride=2), :] = before
        found_rows[pl.ds(32 * l + 21, V, stride=2), :] = last
        found_rows[32 * l + 30 : 32 * l + 32, :] = jnp.zeros((2, N), F32)
        out[l] = found_rows[32 * l : 32 * l + 32, :]
        first, second = [
            offsets[l][j] + packed[:, 16 + 2 * j : 17 + 2 * j] * before
            + packed[:, 17 + 2 * j : 18 + 2 * j] * last
            for j in range(2)
        ]


def sweeps(left_eig, got):
    blocks = got.shape[0]
    return pl.pallas_call(
        functools.partial(sweep_kernel, blocks),
        in_specs=[RESIDENT, RESIDENT],
        out_specs=RESIDENT,
        out_shape=jax.ShapeDtypeStruct((blocks, 32, N), F32),
        scratch_shapes=[
            pltpu.VMEM((blocks * V * ROWS + 8 * ROWS, N), F32),
            pltpu.VMEM((blocks * 32 + 64, N), F32),
        ],
        cost_estimate=pl.CostEstimate(
            flops=2 * 10**9, bytes_accessed=30 * 10**6, transcendentals=0
        ),
        compiler_params=room(32),
        name="sweeps",
    )(left_eig, got)


def coupled_kernel(pattern, base, columns, incoming, out, held, sem):
    def store(g):
        planes = pl.ds(g * LAST_PLANES, LAST_PLANES)
        return pltpu.make_async_copy(held.at[:, planes], out.at[:, planes], sem.at[g])

    def group(g, _):
        for q in range(LAST_PLANES):
            p = g * LAST_PLANES + q
            sides = []
            for u in range(V):
                scaled = incoming[p] * pattern[u]
                high = scaled.astype(BF16)
                low = (scaled - high.astype(F32)).astype(BF16)
                sides.append(jnp.concatenate([high, high, low, low], axis=0))
            change = jnp.dot(columns[p], jnp.concatenate(sides, axis=1), preferred_element_type=F32)
            for u in range(V):
                held[u, p] = base[u, p] + change[:, u * N : (u + 1) * N]
        store(g).start()
        return 0

    lax.fori_loop(0, LAST_GROUPS, group, 0)
    for g in range(LAST_GROUPS):
        store(g).wait()


def coupled(pattern, base, columns, incoming):
    return pl.pallas_call(
        coupled_kernel,
        in_specs=[RESIDENT] * 4,
        out_specs=OUTSIDE,
        out_shape=pltpu.HBM((V, PL, N, N), F32),
        scratch_shapes=[
            pltpu.VMEM((V, PL, N, N), F32),
            pltpu.SemaphoreType.DMA((LAST_GROUPS,)),
        ],
        compiler_params=room(32),
        name="coupled",
    )(pattern, base, columns, incoming)


def local(
    flow_state,
    wave_speed,
    left_eig,
    right_eig,
    lower_inverse,
    upper_inverse,
    lower_link,
    upper_link,
    donor_rows,
    stencil_offsets,
    donor_weights,
    block_counts,
    receptor_rows,
):
    flat = flow_state.reshape(V, PL * N, N)
    outgoing = gather_donors(donor_rows, stencil_offsets, donor_weights, flat)
    received = lax.all_to_all(outgoing, "plane", 0, 0, tiled=True)
    rows = receptor_rows.reshape(8, 32)
    valid = jnp.arange(32, dtype=jnp.int32)[None, :] < block_counts.reshape(8, 1)
    target = jnp.where(valid, (rows // N) * PAD + rows % N + 8, SPARE)
    lower_inverse, outgoing = lax.optimization_barrier((lower_inverse, outgoing))
    both_parts, edge_rows, columns, early, pattern = factors(
        lower_inverse,
        upper_inverse,
        wave_speed,
        lower_link.reshape(3, V, PL, N),
        upper_link.reshape(3, V, PL, N),
        right_eig,
    )
    tend, patched, edges = stencil(
        target,
        left_eig,
        received,
        flow_state,
        wave_speed,
        edge_rows,
        early,
    )
    edges = edges.reshape(PL, V * ROWS, N)
    got = lax.all_to_all(edges, "line", 0, 0, tiled=True)
    base = uncoupled(left_eig, right_eig, both_parts, tend, patched)
    got, base = lax.optimization_barrier((got, base))
    incoming = lax.all_to_all(sweeps(left_eig, got), "line", 0, 0, tiled=True)
    return coupled(pattern, base, columns, incoming)


def solution(mesh):
    in_specs = (
        P(None, "plane", "line", None),
        P("plane", "line", None),
        P(),
        P(),
        P(None, "plane", "line", None),
        P(None, "plane", "line", None),
        P(None, None, "plane", "line", None),
        P(None, None, "plane", "line", None),
        P("plane", "line", None, None),
        P("plane", "line", None, None),
        P(None, "plane", "line", None, None),
        P(None, "line", "plane"),
        P("plane", "line", None, None),
    )
    out_specs = P(None, "plane", "line", None)
    return jax.shard_map(local, mesh=mesh, in_specs=in_specs, out_specs=out_specs, check_vma=False)
```

```python
import functools

import jax
import jax.numpy as jnp
from jax import lax
from jax.experimental import pallas as pl
from jax.experimental.pallas import tpu as pltpu
from jax.sharding import PartitionSpec as P

F32 = jnp.float32
BF16 = jnp.bfloat16
V = 5
PL = 16
N = 128
PAD = 144
SPARE = 143
ROWS = 16
EDGES = (126, 127, 0, 1)
PAIR = 2
GROUPS = PL // PAIR
LAST_PLANES = 4
LAST_GROUPS = PL // LAST_PLANES
VARIABLE_GROUPS = ((0, 1), (2, 3, 4))
BATCH = 4
AHEAD = 3
SCALARS = pl.BlockSpec(memory_space=pltpu.SMEM)
RESIDENT = pl.BlockSpec(memory_space=pltpu.VMEM)
OUTSIDE = pl.BlockSpec(memory_space=pl.ANY)


def room(mebibytes):
    return pltpu.CompilerParams(vmem_limit_bytes=mebibytes * 2**20)


def in_hbm(x):
    return pltpu.with_memory_space_constraint(x, pltpu.HBM)


def split(x):
    high = x.astype(BF16)
    low = (x - high.astype(F32)).astype(BF16)
    return jnp.concatenate([high, low], axis=1)


def product(left_parts, right_parts):
    both = jnp.concatenate([right_parts, right_parts], axis=0)
    wide = jnp.dot(left_parts, both, preferred_element_type=F32)
    return wide[:, :N] + wide[:, N:]


def gather_kernel(
    rows_in, offsets_in, weights_in, flow, out,
    rows, offsets, weights, held, found, scalar_sem, sem, store_sem,
):
    groups = ((0,), (1, 2), (3, 4))
    scalars = [
        pltpu.make_async_copy(source, to, scalar_sem.at[i])
        for i, (source, to) in enumerate(
            ((rows_in, rows), (offsets_in, offsets), (weights_in, weights))
        )
    ]
    for copy in scalars:
        copy.start()

    def load(v):
        return pltpu.make_async_copy(flow.at[v], held.at[v, pl.ds(0, PL * N)], sem.at[v])

    def store(d, k):
        part = pl.ds(groups[k][0], len(groups[k]))
        return pltpu.make_async_copy(found.at[d, part], out.at[d, part], store_sem.at[k, d])

    for v in range(V):
        load(v).start()
    for copy in scalars:
        copy.wait()
    for k, group in enumerate(groups):
        for v in group:
            load(v).wait()

        def peer(d, _):
            for c in range(32):
                first = rows[0, 0, d, c]
                second = first + offsets[0, 0, d, c]
                near, far = weights[0, 0, 0, d, c], weights[1, 0, 0, d, c]
                for v in group:
                    found[d, v, pl.ds(c, 1), :] = (
                        near * held[v, pl.ds(first, 1), :] + far * held[v, pl.ds(second, 1), :]
                    )
            store(d, k).start()
            return 0

        lax.fori_loop(0, 8, peer, 0)
    for k in range(3):
        for d in range(8):
            store(d, k).wait()


def gather_donors(donor_rows, stencil_offsets, donor_weights, flat):
    return pl.pallas_call(
        gather_kernel,
        in_specs=[OUTSIDE] * 4,
        out_specs=OUTSIDE,
        out_shape=pltpu.HBM((8, V, 32, N), F32),
        scratch_shapes=[
            pltpu.SMEM((1, 1, 8, 32), jnp.int32),
            pltpu.SMEM((1, 1, 8, 32), jnp.int32),
            pltpu.SMEM((2, 1, 1, 8, 32), F32),
            pltpu.VMEM((V, PL * N + 8, N), F32),
            pltpu.VMEM((8, V, 32, N), F32),
            pltpu.SemaphoreType.DMA((3,)),
            pltpu.SemaphoreType.DMA((V,)),
            pltpu.SemaphoreType.DMA((3, 8)),
        ],
        compiler_params=room(56),
        cost_estimate=pl.CostEstimate(flops=10**6, bytes_accessed=6 * 10**6, transcendentals=0),
        name="gather_donors",
    )(donor_rows, stencil_offsets, donor_weights, in_hbm(flat))


def factors_kernel(
    lower, upper, wave, lower_link, upper_link, right_eig,
    both_out, edge_rows, columns, early, pattern,
    lows, ups, both_parts, load_sem, store_sem,
):
    def loads(g):
        planes = pl.ds(g * PAIR, PAIR)
        return [
            pltpu.make_async_copy(source.at[:, planes], held.at[:, planes], load_sem.at[k, g])
            for k, (source, held) in enumerate(((lower, lows), (upper, ups)))
        ]

    def store(g):
        planes = pl.ds(g * PAIR, PAIR)
        return pltpu.make_async_copy(
            both_parts.at[:, planes], both_out.at[:, planes], store_sem.at[g]
        )

    for g in range(AHEAD):
        for copy in loads(g):
            copy.start()
    for u in range(V):
        for v in range(V):
            pattern[u, 4 * v : 4 * v + 4, :] = jnp.full((4, N), right_eig[u, v])
            pattern[u, 20 + 2 * v : 22 + 2 * v, :] = jnp.full((2, N), right_eig[u, v])
        pattern[u, 30:32, :] = jnp.zeros((2, N), F32)
    lane = lax.broadcasted_iota(jnp.int32, (N, N), 1)
    lane_row = lax.broadcasted_iota(jnp.int32, (1, N), 1)

    def group(g, _):
        @pl.when(g + AHEAD < GROUPS)
        def _():
            for copy in loads(g + AHEAD):
                copy.start()

        for copy in loads(g):
            copy.wait()
        for q in range(PAIR):
            p = g * PAIR + q
            cols = jnp.zeros((N, N), F32)
            ends = []
            for v in range(V):
                low, up = lows[v, p], ups[v, p]
                both = product(split(up), split(low))
                both_parts[v, p] = split(both)
                ends += [both[0:2], low[126:128]]
                at = 4 * v
                cols = jnp.where((lane >= at) & (lane < at + 4), pltpu.roll(both, at + 2, axis=1), cols)
                at = 20 + 2 * v
                cols = jnp.where((lane >= at) & (lane < at + 2), pltpu.roll(up, at + 2, axis=1), cols)
                packed = jnp.zeros((1, N), F32)
                for i, row in enumerate((both[0:1], both[1:2], low[126:127], low[127:128])):
                    at = 4 * i
                    packed = jnp.where(
                        (lane_row >= at) & (lane_row < at + 4), pltpu.roll(row, at + 2, axis=1), packed
                    )
                for i, row in enumerate((up[0:1], up[1:2])):
                    at = 16 + 2 * i
                    packed = jnp.where(
                        (lane_row >= at) & (lane_row < at + 2), pltpu.roll(row, at + 2, axis=1), packed
                    )
                for i in range(3):
                    early[p, v, i : i + 1, :] = lower_link[i, v, pl.ds(p, 1), :]
                    early[p, v, 3 + i : 4 + i, :] = upper_link[i, v, pl.ds(p, 1), :]
                point = EDGES[min(v, 3)]
                early[p, v, 6:7, :] = wave[p, point : point + 1, :]
                early[p, v, 7:8, :] = packed
            ends = jnp.concatenate(ends + [jnp.zeros((4, N), F32)], axis=0)
            high = ends.astype(BF16).astype(F32)
            edge_rows[p] = jnp.concatenate([high, ends - high], axis=0).astype(BF16)
            high = cols.astype(BF16).astype(F32)
            pair = high + pltpu.roll(cols - high, 32, axis=1)
            columns[p] = (pair + pltpu.roll(pair, 64, axis=1)).astype(BF16)
        store(g).start()
        return 0

    lax.fori_loop(0, GROUPS, group, 0)
    for g in range(GROUPS):
        store(g).wait()


def factors(lower_inverse, upper_inverse, wave, lower_link, upper_link, right_eig):
    return pl.pallas_call(
        factors_kernel,
        in_specs=[OUTSIDE] * 2 + [RESIDENT] * 3 + [SCALARS],
        out_specs=[OUTSIDE] + [RESIDENT] * 4,
        out_shape=[
            pltpu.HBM((V, PL, N, 2 * N), BF16),
            jax.ShapeDtypeStruct((PL, 48, N), BF16),
            pltpu.HBM((PL, N, N), BF16),
            jax.ShapeDtypeStruct((PL, V, 8, N), F32),
            pltpu.HBM((V, 32, N), F32),
        ],
        scratch_shapes=[
            pltpu.VMEM((V, PL, N, N), F32),
            pltpu.VMEM((V, PL, N, N), F32),
            pltpu.VMEM((V, PL, N, 2 * N), BF16),
            pltpu.SemaphoreType.DMA((2, GROUPS)),
            pltpu.SemaphoreType.DMA((GROUPS,)),
        ],
        compiler_params=room(32),
        cost_estimate=pl.CostEstimate(
            flops=2 * 10**9, bytes_accessed=17 * 10**6, transcendentals=0
        ),
        name="factors",
    )(
        in_hbm(lower_inverse), in_hbm(upper_inverse), wave, lower_link, upper_link, right_eig
    )


def stencil_kernel(
    target_in, eig_in, received, flow, wave, edge_rows, early,
    tend_out, patched, edges_out,
    target, left_eig, grid_rows, tend, parts, pattern, sums, edges,
    scalar_sem, load_sem, tend_sem, patch_sem, edge_sem, early_sem,
):
    def load(v):
        return pltpu.make_async_copy(flow.at[v], grid_rows.at[v, :, pl.ds(8, N), :], load_sem.at[v])

    def store_tend(k, p):
        part = pl.ds(VARIABLE_GROUPS[k][0], len(VARIABLE_GROUPS[k]))
        return pltpu.make_async_copy(tend.at[part, p], tend_out.at[part, p], tend_sem.at[k, p])

    def store_edges(p):
        return pltpu.make_async_copy(edges.at[p], edges_out.at[p, :, 0], edge_sem.at[p])

    def store_patched(v):
        return pltpu.make_async_copy(
            grid_rows.at[v, :, pl.ds(8, N), :], patched.at[v], patch_sem.at[v]
        )

    copies = [
        pltpu.make_async_copy(target_in, target, scalar_sem.at[0]),
        pltpu.make_async_copy(eig_in, left_eig, scalar_sem.at[1]),
    ]
    for copy in copies:
        copy.start()
    for v in range(V):
        load(v).start()
    store_early = pltpu.make_async_copy(early, edges_out.at[:, :, 1], early_sem.at[0])
    store_early.start()
    flat_rows = grid_rows.reshape(V, PL * PAD, N)
    zeros = jnp.zeros((8, N), F32)
    for v in range(V):
        for q in range(PL):
            grid_rows[v, q, 0:8, :] = zeros
            grid_rows[v, q, 136:144, :] = zeros
    for copy in copies:
        copy.wait()
    for u in range(V):
        for v in range(V):
            pattern[u, 4 * v : 4 * v + 4, :] = jnp.full((4, N), left_eig[v, u])
        pattern[u, 20:24, :] = jnp.zeros((4, N), F32)
    lane = lax.broadcasted_iota(jnp.int32, (16, N), 1)

    for k, group in enumerate(VARIABLE_GROUPS):
        first, last = k == 0, k == len(VARIABLE_GROUPS) - 1
        for v in group:
            load(v).wait()

        def place(d, _):
            for c in range(32):
                row = target[d, c]
                for v in group:
                    flat_rows[v, pl.ds(row, 1), :] = received[d, v, pl.ds(c, 1), :]
            return 0

        lax.fori_loop(0, 8, place, 0)
        for v in group:
            store_patched(v).start()

        def tendency(p, slot):
            for start in range(0, N, 16):
                speed = -0.0625 * wave[p, pl.ds(start, 16), :]
                for v in group:
                    at = lambda shift: grid_rows[v, p, pl.ds(8 + start + shift, 16), :]
                    here = at(0)
                    after = jnp.where(lane == N - 1, 0.0, pltpu.roll(here, N - 1, axis=1))
                    before = jnp.where(lane == 0, 0.0, pltpu.roll(here, 1, axis=1))
                    near = (at(1) - 3.0 * at(-1)) + (1.5 * here + 2.0 * (after - before))
                    total = speed * ((at(2) + at(-2)) + 4.0 * near)
                    tend[v, p, pl.ds(start, 16), :] = total
                    parts[slot, v, pl.ds(start, 16), :] = split(total)
            store_tend(k, p).start()

        def block_edges(p, slot):
            total = jnp.zeros((24, N), F32) if first else sums[p]
            for u in group:
                wide = jnp.dot(
                    edge_rows[p], parts[slot, u], preferred_element_type=F32
                )
                found = wide[:, :N] + wide[:, N:]
                total = total + pattern[u] * (found[:24] + found[24:])
            if not last:
                sums[p] = total
            for v in group:
                edges[p, v, 4:6, :] = grid_rows[v, p, 134:136, :]
                edges[p, v, 6:8, :] = grid_rows[v, p, 8:10, :]
            if last:
                for v in range(V):
                    edges[p, v, 0:4, :] = total[4 * v : 4 * v + 4]
                store_edges(p).start()

        def step(i, _):
            before, now = lax.rem(i + 1, 2) * BATCH, lax.rem(i, 2) * BATCH
            for q in range(BATCH):
                block_edges((i - 1) * BATCH + q, before + q)
            for q in range(BATCH):
                tendency(i * BATCH + q, now + q)
            return 0

        for q in range(BATCH):
            tendency(q, q)
        lax.fori_loop(1, PL // BATCH, step, 0)
        for q in range(BATCH):
            block_edges(PL - BATCH + q, (PL // BATCH - 1) % 2 * BATCH + q)
    for p in range(PL):
        for k in range(len(VARIABLE_GROUPS)):
            store_tend(k, p).wait()
        store_edges(p).wait()
    for v in range(V):
        store_patched(v).wait()
    store_early.wait()


def stencil(target, left_eig, received, flow, wave, edge_rows, early):
    return pl.pallas_call(
        stencil_kernel,
        in_specs=[OUTSIDE, OUTSIDE, RESIDENT, OUTSIDE, RESIDENT, RESIDENT, OUTSIDE],
        out_specs=[OUTSIDE] * 3,
        out_shape=[
            pltpu.HBM((V, PL, N, N), F32),
            pltpu.HBM((V, PL, N, N), F32),
            pltpu.HBM((PL, V, 2, 8, N), F32),
        ],
        scratch_shapes=[
            pltpu.SMEM((8, 32), jnp.int32),
            pltpu.SMEM((V, V), F32),
            pltpu.VMEM((V, PL, PAD, N), F32),
            pltpu.VMEM((V, PL, N, N), F32),
            pltpu.VMEM((2 * BATCH, V, N, 2 * N), BF16),
            pltpu.VMEM((V, 24, N), F32),
            pltpu.VMEM((PL, 24, N), F32),
            pltpu.VMEM((PL, V, 8, N), F32),
            pltpu.SemaphoreType.DMA((2,)),
            pltpu.SemaphoreType.DMA((V,)),
            pltpu.SemaphoreType.DMA((len(VARIABLE_GROUPS), PL)),
            pltpu.SemaphoreType.DMA((V,)),
            pltpu.SemaphoreType.DMA((PL,)),
            pltpu.SemaphoreType.DMA((1,)),
        ],
        compiler_params=room(32),
        cost_estimate=pl.CostEstimate(
            flops=10**8, bytes_accessed=18 * 10**6, transcendentals=0
        ),
        name="stencil",
    )(target, left_eig, received, in_hbm(flow), wave, edge_rows, early)


def uncoupled_kernel(
    left_eig, right_eig, both_in, tend_in, patched_in, out, both_parts, tend, base, sem, store_sem
):
    def loads(g):
        planes = pl.ds(g * PAIR, PAIR)
        return [
            pltpu.make_async_copy(source.at[:, planes], held.at[:, planes], sem.at[k, g])
            for k, (source, held) in enumerate(
                ((both_in, both_parts), (tend_in, tend), (patched_in, base))
            )
        ]

    def store(g):
        planes = pl.ds(g * PAIR, PAIR)
        return pltpu.make_async_copy(base.at[:, planes], out.at[:, planes], store_sem.at[g])

    for g in range(AHEAD):
        for copy in loads(g):
            copy.start()

    def group(g, _):
        @pl.when(g + AHEAD < GROUPS)
        def _():
            for copy in loads(g + AHEAD):
                copy.start()

        for copy in loads(g):
            copy.wait()
        for q in range(PAIR):
            p = g * PAIR + q
            solved = []
            for v in range(V):
                total = left_eig[v, 0] * tend[0, p]
                for u in range(1, V):
                    total = total + left_eig[v, u] * tend[u, p]
                solved.append(product(both_parts[v, p], split(total)))
            for u in range(V):
                total = base[u, p]
                for v in range(V):
                    total = total + right_eig[u, v] * solved[v]
                base[u, p] = total
        store(g).start()
        return 0

    lax.fori_loop(0, GROUPS, group, 0)
    for g in range(GROUPS):
        store(g).wait()


def uncoupled(left_eig, right_eig, both_parts, tend, patched):
    return pl.pallas_call(
        uncoupled_kernel,
        in_specs=[SCALARS, SCALARS, OUTSIDE, OUTSIDE, OUTSIDE],
        out_specs=OUTSIDE,
        out_shape=pltpu.HBM((V, PL, N, N), F32),
        scratch_shapes=[
            pltpu.VMEM((V, PL, N, 2 * N), BF16),
            pltpu.VMEM((V, PL, N, N), F32),
            pltpu.VMEM((V, PL, N, N), F32),
            pltpu.SemaphoreType.DMA((3, GROUPS)),
            pltpu.SemaphoreType.DMA((GROUPS,)),
        ],
        compiler_params=room(32),
        cost_estimate=pl.CostEstimate(
            flops=2 * 10**9, bytes_accessed=21 * 10**6, transcendentals=0
        ),
        name="uncoupled",
    )(left_eig, right_eig, in_hbm(both_parts), in_hbm(tend), in_hbm(patched))


def sweep_kernel(blocks, left_eig, got, out, rows, found_rows):
    height = V * ROWS
    for l in range(blocks):
        rows[l * height : (l + 1) * height, :] = got[l]
    take = lambda l, j: rows[pl.ds(l * height + j, V, stride=ROWS), :]
    zero = jnp.zeros((V, N), F32)
    eig = [jnp.broadcast_to(left_eig[:, u : u + 1], (V, N)) for u in range(V)]

    def mixed(tendency):
        total = eig[0] * tendency[0:1]
        for u in range(1, V):
            total = total + eig[u] * tendency[u : u + 1]
        return total

    first, second = zero, zero
    offsets = []
    for l in range(blocks):
        speed = {
            e: -0.0625 * got[l, ROWS * i + 14 : ROWS * i + 15, :] for i, e in enumerate(EDGES)
        }
        packed = take(l, 15)
        scalar = lambda k: packed[:, k : k + 1]
        edge = {e: zero for e in EDGES}
        if l > 0:
            far, near = take(l - 1, 4), take(l - 1, 5)
            edge[0] = mixed(speed[0] * (far - 12.0 * near))
            edge[1] = mixed(speed[1] * near)
        if l < blocks - 1:
            near, far = take(l + 1, 6), take(l + 1, 7)
            edge[126] = mixed(speed[126] * near)
            edge[127] = mixed(speed[127] * (far + 4.0 * near))
        edge[0] = edge[0] - (take(l, 8) * first + take(l, 9) * second)
        edge[1] = edge[1] - take(l, 10) * first
        for i, e in enumerate(EDGES):
            found_rows[pl.ds(32 * l + i, V, stride=4), :] = edge[e]
        found = []
        for j in range(4):
            total = take(l, j)
            for i, e in enumerate(EDGES):
                total = total + scalar(4 * j + i) * edge[e]
            found.append(total)
        offsets.append(found[:2])
        first, second = found[3], found[2]
    first, second = zero, zero
    for l in range(blocks - 1, -1, -1):
        packed = take(l, 15)
        last = -(take(l, 11) * first + take(l, 12) * second)
        before = -(take(l, 13) * first)
        found_rows[pl.ds(32 * l + 20, V, stride=2), :] = before
        found_rows[pl.ds(32 * l + 21, V, stride=2), :] = last
        found_rows[32 * l + 30 : 32 * l + 32, :] = jnp.zeros((2, N), F32)
        out[l] = found_rows[32 * l : 32 * l + 32, :]
        first, second = [
            offsets[l][j] + packed[:, 16 + 2 * j : 17 + 2 * j] * before
            + packed[:, 17 + 2 * j : 18 + 2 * j] * last
            for j in range(2)
        ]


def sweeps(left_eig, got):
    blocks = got.shape[0]
    return pl.pallas_call(
        functools.partial(sweep_kernel, blocks),
        in_specs=[RESIDENT, RESIDENT],
        out_specs=RESIDENT,
        out_shape=jax.ShapeDtypeStruct((blocks, 32, N), F32),
        scratch_shapes=[
            pltpu.VMEM((blocks * V * ROWS + 8 * ROWS, N), F32),
            pltpu.VMEM((blocks * 32 + 64, N), F32),
        ],
        cost_estimate=pl.CostEstimate(
            flops=2 * 10**9, bytes_accessed=30 * 10**6, transcendentals=0
        ),
        compiler_params=room(32),
        name="sweeps",
    )(left_eig, got)


def coupled_kernel(pattern, base, columns, incoming, out, held, sem):
    def store(g):
        planes = pl.ds(g * LAST_PLANES, LAST_PLANES)
        return pltpu.make_async_copy(held.at[:, planes], out.at[:, planes], sem.at[g])

    def group(g, _):
        for q in range(LAST_PLANES):
            p = g * LAST_PLANES + q
            sides = []
            for u in range(V):
                scaled = incoming[p] * pattern[u]
                high = scaled.astype(BF16)
                low = (scaled - high.astype(F32)).astype(BF16)
                sides.append(jnp.concatenate([high, high, low, low], axis=0))
            change = jnp.dot(columns[p], jnp.concatenate(sides, axis=1), preferred_element_type=F32)
            for u in range(V):
                held[u, p] = base[u, p] + change[:, u * N : (u + 1) * N]
        store(g).start()
        return 0

    lax.fori_loop(0, LAST_GROUPS, group, 0)
    for g in range(LAST_GROUPS):
        store(g).wait()


def coupled(pattern, base, columns, incoming):
    return pl.pallas_call(
        coupled_kernel,
        in_specs=[RESIDENT] * 4,
        out_specs=OUTSIDE,
        out_shape=pltpu.HBM((V, PL, N, N), F32),
        scratch_shapes=[
            pltpu.VMEM((V, PL, N, N), F32),
            pltpu.SemaphoreType.DMA((LAST_GROUPS,)),
        ],
        compiler_params=room(32),
        name="coupled",
    )(pattern, base, columns, incoming)


def local(
    flow_state,
    wave_speed,
    left_eig,
    right_eig,
    lower_inverse,
    upper_inverse,
    lower_link,
    upper_link,
    donor_rows,
    stencil_offsets,
    donor_weights,
    block_counts,
    receptor_rows,
):
    flat = flow_state.reshape(V, PL * N, N)
    outgoing = gather_donors(donor_rows, stencil_offsets, donor_weights, flat)
    received = lax.all_to_all(outgoing, "plane", 0, 0, tiled=True)
    rows = receptor_rows.reshape(8, 32)
    valid = jnp.arange(32, dtype=jnp.int32)[None, :] < block_counts.reshape(8, 1)
    target = jnp.where(valid, (rows // N) * PAD + rows % N + 8, SPARE)
    lower_inverse, outgoing = lax.optimization_barrier((lower_inverse, outgoing))
    both_parts, edge_rows, columns, early, pattern = factors(
        lower_inverse,
        upper_inverse,
        wave_speed,
        lower_link.reshape(3, V, PL, N),
        upper_link.reshape(3, V, PL, N),
        right_eig,
    )
    tend, patched, edges = stencil(
        target,
        left_eig,
        received,
        flow_state,
        wave_speed,
        edge_rows,
        early,
    )
    edges = edges.reshape(PL, V * ROWS, N)
    got = lax.all_to_all(edges, "line", 0, 0, tiled=True)
    base = uncoupled(left_eig, right_eig, both_parts, tend, patched)
    got, base = lax.optimization_barrier((got, base))
    incoming = lax.all_to_all(sweeps(left_eig, got), "line", 0, 0, tiled=True)
    return coupled(pattern, base, columns, incoming)


def solution(mesh):
    in_specs = (
        P(None, "plane", "line", None),
        P("plane", "line", None),
        P(),
        P(),
        P(None, "plane", "line", None),
        P(None, "plane", "line", None),
        P(None, None, "plane", "line", None),
        P(None, None, "plane", "line", None),
        P("plane", "line", None, None),
        P("plane", "line", None, None),
        P(None, "plane", "line", None, None),
        P(None, "line", "plane"),
        P("plane", "line", None, None),
    )
    out_specs = P(None, "plane", "line", None)
    return jax.shard_map(local, mesh=mesh, in_specs=in_specs, out_specs=out_specs, check_vma=False)
```
